512 devices in a mesh: grp: 4 (over z_hi), slab: 128 (over y, z_lo, x, core).
Axes of the slice: x: 4, y: 8, z: 8 (z_hi: 4, z_lo: 2; z = z_hi * 2 + z_lo), core: 2. Of those that a mesh axis runs over, the one named last changes fastest.
Arguments:
- points: bfloat16 [128, 4, 3072, 96], P('slab', 'grp'), may hold values from -6 to 6
- slot_mask: int32 [128, 4, 3072], P('slab', 'grp'), may hold values from 0 to 1, as said below
- window_counts: int32 [128, 4], P('slab', 'grp'), may hold values from 24 to 96
- block_gains: float32 [2, 2, 96], replicated, may hold values from 0.25 to 1.75
- qkv_weight: bfloat16 [2, 96, 288], replicated, may hold values from -1 to 1
- out_weight: bfloat16 [2, 96, 96], replicated, may hold values from -0.625 to 0.625
- mlp_in: bfloat16 [2, 96, 384], replicated, may hold values from -0.625 to 0.625
- mlp_out: bfloat16 [2, 384, 96], replicated, may hold values from -0.3125 to 0.3125
- down_weight: bfloat16 [768, 192], replicated, may hold values from -0.21875 to 0.21875
- coarse_gain: float32 [192], replicated, may hold values from 0.25 to 1.75
- coarse_grad: bfloat16 [128, 1536, 192], P('slab'), may hold values from -6 to 6
Outputs:
- coarse: bfloat16 [128, 1536, 192], P('slab')
- fine_grad: bfloat16 [128, 4, 3072, 96], P('slab', 'grp')
- down_grad: float32 [768, 192], replicated
The draws below stay inside these ranges and needn't reach their ends.
Inputs may be any that keep to these rules, and one draw needn't show every extreme that they name: `slot_mask`: each run of 8 aligned slots holds at least one 1.
All inputs are finite; a program needn't handle non-finite values.
Results may differ from the reference program's by a relative error of at most 0.012.
Values may be sent and summed in bfloat16 or wider, within the bound.
A program may use at most 128 MiB of HBM per device.

```python
import math
import jax
import jax.numpy as jnp
from jax import lax

C = 96
C2 = 192
HEADS = 6
FFN = 384
WINDOW = 32
PARENT = 8
W_DEV = 96
ROWS = 3072
CROWS = 1536
N_GRP = 4
N_SLAB = 128


def draw_points(key, part):
    key = jax.random.fold_in(key, 5)
    base_key = jax.random.fold_in(key, 0)
    full_shape = (N_SLAB, N_GRP, ROWS, C)
    drawn = jax.random.truncated_normal(base_key, -6.0, 6.0, full_shape, jnp.float32)
    return drawn.astype(jnp.bfloat16)


def draw_qkv_weight(key, part):
    key = jax.random.fold_in(key, 7)
    full_shape = (2, C, 3 * C)
    spread_w = C ** (-0.5)
    drawn = jax.random.truncated_normal(key, -3.0, 3.0, full_shape, jnp.float32) * spread_w
    return drawn.astype(jnp.bfloat16)


def draw_slot_mask(key, part):
    key = jax.random.fold_in(key, 11)
    first, second = jax.random.split(key)
    count = N_SLAB * N_GRP * W_DEV * WINDOW // PARENT
    extra = jax.random.randint(first, (count, PARENT), 0, 20) < 11
    anchor = jax.random.randint(second, (count, 1), 0, PARENT)
    held = extra | (jnp.arange(PARENT, dtype=jnp.int32)[None, :] == anchor)
    return held.astype(jnp.int32).reshape(N_SLAB, N_GRP, W_DEV * WINDOW)


def draw_window_counts(key, part):
    key = jax.random.fold_in(key, 23)
    first, second, third = jax.random.split(key, 3)
    total = N_SLAB * N_GRP
    lowest = max(W_DEV // 4, 1)
    counts = jax.random.randint(first, (total,), lowest, W_DEV + 1)
    highest_at = jax.random.randint(second, (), 0, total)
    lowest_at = (highest_at + jax.random.randint(third, (), 1, total)) % total
    counts = counts.at[highest_at].set(W_DEV).at[lowest_at].set(lowest)
    return counts.astype(jnp.int32).reshape(N_SLAB, N_GRP)


def shard_levels(own_key, extent, cuts, low, high):
    level, own = 1.0, jax.random.fold_in(own_key, 6)
    for axis_at, parts in cuts:
        draws = jnp.exp(jax.random.uniform(jax.random.fold_in(own, axis_at), (parts,), jnp.float32, low / len(cuts), high / len(cuts)))
        level = level * jnp.repeat(draws, extent[axis_at] // parts).reshape([-1 if axis == axis_at else 1 for axis in range(len(extent))])
    return level


def gaussian(own_key, shape, deviation, bound, cuts=(), kind=jnp.bfloat16):
    entries = jax.random.normal(own_key, shape, jnp.float32) * deviation
    if len(cuts) > 0:
        entries = shard_levels(own_key, shape, cuts, -0.22, 0.18) * entries
    return jnp.clip(entries, min=-bound, max=bound).astype(kind)


def setup_inputs(seed: int = 0) -> dict:
    splits = jax.random.split(jax.random.key(seed), 12)
    return {
        "points": draw_points(jax.random.fold_in(splits[11], 71), 0),
        "slot_mask": draw_slot_mask(jax.random.fold_in(splits[11], 71), 0),
        "window_counts": draw_window_counts(jax.random.fold_in(splits[11], 71), 0),
        "block_gains": jnp.clip(1.0 + 0.15 * jax.random.normal(splits[3], (2, 2, C), jnp.float32), 0.25, 1.75),
        "qkv_weight": draw_qkv_weight(jax.random.fold_in(splits[11], 71), 0),
        "out_weight": gaussian(splits[5], (2, C, C), C ** -0.5, 0.625),
        "mlp_in": gaussian(splits[6], (2, C, FFN), C ** -0.5, 0.625),
        "mlp_out": gaussian(splits[7], (2, FFN, C), FFN ** -0.5, 0.3125),
        "down_weight": gaussian(splits[8], (PARENT * C, C2), (PARENT * C) ** -0.5, 0.21875),
        "coarse_gain": jnp.clip(1.0 + 0.15 * jax.random.normal(splits[9], (C2,), jnp.float32), 0.25, 1.75),
        "coarse_grad": gaussian(splits[10], (N_SLAB, CROWS, C2), 1.0, 6.0, ((0, 128),)),
    }


EPS = 1e-05
NEG = -1e+30

def layer_norm(value, gain):
    mean = lax.optimization_barrier(jnp.mean(value, -1, keepdims=True))
    centered = value - mean
    spread = lax.optimization_barrier(jnp.mean(centered * centered, -1, keepdims=True))
    return centered * lax.rsqrt(spread + EPS) * gain

def attend(query, keys, values, include):
    width = query.shape[-1]
    depth = width // HEADS
    query_h = query.reshape(query.shape[:-1] + (HEADS, depth)).astype(jnp.float32)
    keys_h = keys.reshape(keys.shape[:-1] + (HEADS, depth)).astype(jnp.float32)
    values_h = values.reshape(values.shape[:-1] + (HEADS, depth)).astype(jnp.float32)
    scores = jnp.einsum('...qhd,...khd->...hqk', query_h, keys_h) * float(depth) ** (-0.5)
    seen = include[..., None, :, :]
    masked = jnp.where(seen, scores, NEG)
    top = lax.optimization_barrier(jnp.max(masked, -1, keepdims=True))
    expo = jnp.where(seen, jnp.exp(masked - top), 0.0)
    weights = (expo / lax.optimization_barrier(jnp.sum(expo, -1, keepdims=True))).astype(jnp.bfloat16)
    result = jnp.einsum('...hqk,...khd->...qhd', weights.astype(jnp.float32), values_h)
    return result.reshape(query.shape[:-1] + (width,)).astype(jnp.bfloat16)

def run_block(state, live, gains, w_qkv, w_out, w_in, w_back, dilated):
    groups, rows, width = state.shape
    windows = rows // WINDOW
    per_set = WINDOW // groups
    normed = layer_norm(state, gains[0]).astype(jnp.bfloat16)
    qkv = jnp.dot(normed, w_qkv, preferred_element_type=jnp.float32).astype(jnp.bfloat16)
    if dilated:
        sets = qkv.reshape(groups, windows, per_set, groups, 3 * width)
        sets = jnp.transpose(sets, (1, 3, 0, 2, 4)).reshape(windows, groups, WINDOW, 3 * width)
        set_live = live.reshape(groups, windows, per_set, groups)
        set_live = jnp.transpose(set_live, (1, 3, 0, 2)).reshape(windows, groups, 1, WINDOW)
        keep = (set_live > 0.5) | jnp.eye(WINDOW, dtype=bool)
        result = attend(sets[..., :width], sets[..., width:2 * width], sets[..., 2 * width:], keep)
        result = result.reshape(windows, groups, groups, per_set, width)
        heads_out = jnp.transpose(result, (2, 0, 3, 1, 4)).reshape(groups, rows, width)
    else:
        sets = qkv.reshape(groups, windows, WINDOW, 3 * width)
        keep = (live.reshape(groups, windows, 1, WINDOW) > 0.5) | jnp.eye(WINDOW, dtype=bool)
        result = attend(sets[..., :width], sets[..., width:2 * width], sets[..., 2 * width:], keep)
        heads_out = result.reshape(groups, rows, width)
    state = state + jnp.dot(heads_out, w_out, preferred_element_type=jnp.float32)
    inner = layer_norm(state, gains[1]).astype(jnp.bfloat16)
    hidden = jax.nn.gelu(jnp.dot(inner, w_in, preferred_element_type=jnp.float32), approximate=False).astype(jnp.bfloat16)
    return state + jnp.dot(hidden, w_back, preferred_element_type=jnp.float32)

def reference(points, slot_mask, window_counts, block_gains, qkv_weight, out_weight, mlp_in, mlp_out, down_weight, coarse_gain, coarse_grad):
    groups = points.shape[1]
    rows = points.shape[2]
    width = points.shape[3]
    wide = down_weight.shape[1]
    slot_window = jnp.arange(rows, dtype=jnp.int32) // WINDOW

    def one_slab(total, inputs):
        feats, mask, counts, cot = inputs
        live = mask.astype(jnp.float32) * (slot_window[None, :] < counts[:, None]).astype(jnp.float32)
        state = feats.astype(jnp.float32)
        for index in range(2):
            state = run_block(state, live, block_gains[index], qkv_weight[index], out_weight[index], mlp_in[index], mlp_out[index], index == 1)
        fine = state.astype(jnp.bfloat16)
        pooled = (fine * live[..., None].astype(jnp.bfloat16)).reshape(groups, rows // PARENT, PARENT * width)
        pre = jnp.dot(pooled, down_weight, preferred_element_type=jnp.float32)

        def coarse_map(value):
            return layer_norm(value, coarse_gain)
        normed, pullback = jax.vjp(coarse_map, pre)
        coarse_run = normed.astype(jnp.bfloat16).reshape(groups * rows // PARENT, wide)
        d_pre, = pullback(cot.astype(jnp.float32).reshape(groups, rows // PARENT, wide))
        flat_pooled = pooled.reshape(groups * rows // PARENT, PARENT * width)
        d_half = d_pre.reshape(groups * rows // PARENT, wide).astype(jnp.bfloat16)
        term = lax.dot_general(flat_pooled, d_half, (((0,), (0,)), ((), ())), preferred_element_type=jnp.float32)
        back = lax.dot_general(d_half, down_weight, (((1,), (1,)), ((), ())), preferred_element_type=jnp.float32)
        fine_grad = (back.reshape(groups, rows, width) * live[..., None]).astype(jnp.bfloat16)
        return (total + term, (coarse_run, fine_grad))
    start = jnp.zeros((PARENT * width, wide), jnp.float32)
    total, (coarse, fine_grad) = lax.scan(one_slab, start, (points, slot_mask, window_counts, coarse_grad))
    down_grad = total * (1.0 / math.sqrt(N_SLAB * CROWS))
    return (coarse, fine_grad, down_grad)
```

```python
import functools
import math

import jax
import jax.numpy as jnp
from jax import lax
from jax.experimental import pallas as pl
from jax.experimental.pallas import tpu as pltpu
from jax.sharding import PartitionSpec as P

MESH = pl.DeviceIdType.MESH
F32 = jnp.float32
BF = jnp.bfloat16
HEADS = 6
DEPTH = 16
WIDTH = 96
WINDOW = 32
LANES = 128
CHUNK = 512
PARENT = 8
WIDE = 192
EPS = 1e-05
NEG = -1e30
VMEM_LIMIT = 56 * 1024 * 1024


def dot(a, b, ca, cb):
    return lax.dot_general(a, b, (((ca,), (cb,)), ((), ())), preferred_element_type=F32)


def iota(shape, dim):
    return lax.broadcasted_iota(jnp.int32, shape, dim)


def place_of(slot):
    window, cell, odd, member = slot // 32, (slot % 32) // 8, (slot % 8) // 4, slot % 4
    return member * 32 + window * 8 + odd * 4 + cell


def onehot(rows, cols, match):
    return jnp.where(match(iota((rows, cols), 0), iota((rows, cols), 1)), 1.0, 0.0).astype(BF)


def deal_matrix():
    return onehot(LANES, LANES, lambda s, l: place_of(s) == l)


def cell_matrix():
    def match(r, l):
        child, cell = r // 16, r % 16
        return place_of((cell // 4) * 32 + (cell % 4) * 8 + child) == l

    return onehot(LANES, LANES, match)


def norm_rows(value, gain):
    mean = jnp.mean(value, axis=0, keepdims=True)
    centered = value - mean
    spread = jnp.mean(centered * centered, axis=0, keepdims=True)
    return centered * lax.rsqrt(spread + EPS) * gain


def gelu(x):
    return 0.5 * x * (1.0 + lax.erf(x * (0.5**0.5)))


def key_mask(live_row):
    key = iota((WINDOW, LANES), 0)
    lane = iota((WINDOW, LANES), 1)
    own = (lane // 32) * 8 + lane % 8 == key
    spread = jnp.where(own, jnp.broadcast_to(live_row, (WINDOW, LANES)), 0.0).astype(BF)
    same = onehot(LANES, LANES, lambda a, b: (a % 32) // 8 == (b % 32) // 8)
    seen = dot(spread, same, 1, 0)
    return (seen > 0.5) | own


def attend(qkv_t, live_row):
    keys = jnp.transpose(qkv_t[WIDTH : 2 * WIDTH].astype(F32)).astype(BF)
    mask = key_mask(live_row)
    mask2 = jnp.concatenate([mask, mask], 1)
    which = (iota((1, 1, 2 * LANES), 2) % 32) // 8
    outs = []
    for pair in range(HEADS // 2):
        zero = jnp.zeros((DEPTH, LANES), BF)
        cols = []
        for h in (2 * pair, 2 * pair + 1):
            q = qkv_t[h * DEPTH : (h + 1) * DEPTH]
            cols.append(jnp.concatenate([q if i == h else zero for i in range(HEADS)], 0))
        queries = jnp.concatenate(cols, 1)
        scores = dot(keys, queries, 1, 0).reshape(4, 4, 8, 2 * LANES)
        folded = jnp.where(
            which == 0,
            scores[:, 0],
            jnp.where(which == 1, scores[:, 1], jnp.where(which == 2, scores[:, 2], scores[:, 3])),
        ).reshape(WINDOW, 2 * LANES)
        folded = jnp.where(mask2, folded, NEG)
        top = jnp.max(folded, axis=0, keepdims=True)
        expo = jnp.exp(folded - top)
        total = jnp.sum(expo, axis=0, keepdims=True)
        weights = (expo / total).reshape(4, 8, 2 * LANES)
        spread = jnp.stack([jnp.where(which == w, weights, 0.0) for w in range(4)], 1)
        spread = spread.reshape(LANES, 2 * LANES).astype(BF)
        vals = qkv_t[2 * WIDTH + pair * 32 : 2 * WIDTH + pair * 32 + 32]
        mixed = dot(vals, spread, 1, 0)
        outs.append(mixed[:DEPTH, :LANES])
        outs.append(mixed[DEPTH:, LANES:])
    return jnp.concatenate(outs, 0)


def project(w_t, normed, rows_last):
    qkv = dot(w_t, normed, 1, 1 if rows_last else 0)
    return jnp.concatenate([qkv[:WIDTH] * (DEPTH**-0.5), qkv[WIDTH:]], 0).astype(BF)


def feed_forward(state, gain, w_in_t, w_back_t):
    inner = norm_rows(state, gain).astype(BF)
    hidden = gelu(dot(w_in_t, inner, 1, 0)).astype(BF)
    return state + dot(w_back_t, hidden, 1, 0)


def turn(w):
    return jnp.transpose(w.astype(F32)).astype(BF)


def first_kernel(points_ref, live_ref, gains_ref, qkv_ref, out_ref, in_ref, back_ref, state_ref, normed_ref,
                 wq, wo, wi, wb):
    @pl.when(pl.program_id(0) == 0)
    def _():
        wq[...] = turn(qkv_ref[...])
        wo[...] = turn(out_ref[...])
        wi[...] = turn(in_ref[...])
        wb[...] = turn(back_ref[...])

    deal = deal_matrix()
    state = jnp.concatenate(
        [dot(points_ref[b * LANES : (b + 1) * LANES, :], deal, 0, 0) for b in range(4)], 1
    )
    qkv = project(wq[...], norm_rows(state, gains_ref[:, 0:1]).astype(BF), False)
    heads = jnp.concatenate(
        [attend(qkv[:, b * LANES : (b + 1) * LANES], live_ref[0, b : b + 1, :]) for b in range(4)], 1
    ).astype(BF)
    state = state + dot(wo[...], heads, 1, 0)
    state = feed_forward(state, gains_ref[:, 1:2], wi[...], wb[...])
    state_ref[0] = state
    normed = norm_rows(state, gains_ref[:, 2:3])
    for b in range(4):
        rows = jnp.transpose(normed[:, b * LANES : (b + 1) * LANES]).astype(BF)
        for r in range(4):
            normed_ref[r, b] = rows[r * 32 : (r + 1) * 32]


def second_kernel(got_ref, live_ref, qkv_ref, heads_ref, wq):
    @pl.when(pl.program_id(0) == 0)
    def _():
        wq[...] = turn(qkv_ref[...])

    for b in range(4):
        rows = jnp.concatenate([got_ref[g, b] for g in range(4)], 0)
        qkv = project(wq[...], rows, True)
        heads = jnp.transpose(attend(qkv, live_ref[0, b : b + 1, :])).astype(BF)
        for g in range(4):
            heads_ref[g, b] = heads[g * 32 : (g + 1) * 32]


def third_kernel(state_ref, heads_ref, live_ref, gains_ref, out_ref, in_ref, back_ref, pooled_ref, wo, wi, wb):
    @pl.when(pl.program_id(0) == 0)
    def _():
        wo[...] = turn(out_ref[...])
        wi[...] = turn(in_ref[...])
        wb[...] = turn(back_ref[...])

    rows = jnp.concatenate([heads_ref[r, b] for b in range(4) for r in range(4)], 0)
    state = state_ref[0] + dot(wo[...], rows, 1, 1)
    state = feed_forward(state, gains_ref[:, 3:4], wi[...], wb[...])
    deal = cell_matrix()
    for b in range(4):
        fine = state[:, b * LANES : (b + 1) * LANES].astype(BF)
        fine = (fine.astype(F32) * live_ref[0, b : b + 1, :]).astype(BF)
        pooled = dot(deal, fine, 1, 1).astype(BF)
        zero = jnp.zeros((16, LANES - WIDTH), BF)
        for c in range(PARENT):
            pooled_ref[b * 16 : (b + 1) * 16, c * LANES : (c + 1) * LANES] = jnp.concatenate(
                [pooled[c * 16 : (c + 1) * 16], zero], 1
            )


def fourth_kernel(pooled_ref, weight_ref, gain_ref, cot_ref, live_ref, coarse_ref, fine_ref, term_ref, wide, grad):
    cells = pooled_ref.shape[0]
    for c in range(PARENT):
        wide[c * LANES : c * LANES + WIDTH, :] = weight_ref[c * WIDTH : (c + 1) * WIDTH, :]
        wide[c * LANES + WIDTH : (c + 1) * LANES, :] = jnp.zeros((LANES - WIDTH, WIDE), BF)
    pooled = pooled_ref[...]
    weight = wide[...]
    gain = gain_ref[...]
    pre = dot(pooled, weight, 1, 0)
    mean = jnp.mean(pre, -1, keepdims=True)
    centered = pre - mean
    spread = jnp.mean(centered * centered, -1, keepdims=True)
    scale = lax.rsqrt(spread + EPS)
    unit = centered * scale
    coarse_ref[...] = (unit * gain).astype(BF)
    slope = cot_ref[...].astype(F32) * gain
    slope = slope - jnp.mean(slope, -1, keepdims=True) - unit * jnp.mean(slope * unit, -1, keepdims=True)
    half = (slope * scale).astype(BF)
    term = dot(half, pooled, 0, 0).astype(BF)
    for c in range(PARENT):
        term_ref[c] = term[:, c * LANES : (c + 1) * LANES]
    back = dot(half, weight, 1, 1)
    for c in range(PARENT):
        part = back[:, c * LANES : (c + 1) * LANES] * live_ref[:, c : c + 1]
        grad[pl.ds(c, cells, stride=PARENT), :] = part
    fine_ref[...] = grad[:, :WIDTH].astype(BF)


def axis_ids():
    slab, grp = lax.axis_index("slab"), lax.axis_index("grp")
    core, x, z_lo, y = slab % 2, (slab // 2) % 4, (slab // 8) % 2, slab // 16
    return core, x, y, grp * 2 + z_lo


def device_at(core, x, y, z):
    return {"slab": ((y * 2 + z % 2) * 4 + x) * 2 + core, "grp": z // 2}


def meet(peers):
    barrier = pltpu.get_barrier_semaphore()
    for peer in peers:
        pl.semaphore_signal(barrier, inc=1, device_id=peer, device_id_type=MESH)
    pl.semaphore_wait(barrier, len(peers))


def group_peers():
    slab, grp = lax.axis_index("slab"), lax.axis_index("grp")
    return [{"slab": slab, "grp": (grp + d) % 4} for d in (1, 2, 3)]


def send(src, dst, send_sem, recv_sem, peer):
    return pltpu.make_async_remote_copy(
        src_ref=src, dst_ref=dst, send_sem=send_sem, recv_sem=recv_sem, device_id=peer, device_id_type=MESH
    )


def deal_kernel(src_ref, dst_ref, local_sem, send_sem, recv_sem):
    me = lax.axis_index("grp")
    meet(group_peers())
    copies = []
    for d, peer in zip((2, 1, 3), [group_peers()[i] for i in (1, 0, 2)]):
        copies.append(send(src_ref.at[peer["grp"]], dst_ref.at[me], send_sem.at[d - 1], recv_sem.at[d - 1], peer))
        copies[-1].start()
    own = pltpu.make_async_copy(src_ref.at[me], dst_ref.at[me], local_sem)
    own.start()
    own.wait()
    for copy in copies:
        copy.wait()


def share_kernel(coarse_ref, term_ref, run_ref, grad_ref, half, crossed, summed, lines, mine, planes, pieces, column,
                 level, whole, local_sem, run_send, run_recv, sems):
    core, x, y, z = axis_ids()
    me = lax.axis_index("grp")
    cells = coarse_ref.shape[0]
    others = group_peers()
    across = device_at(1 - core, x, y, z)
    beside = [device_at(core, (x + d) % 4, y, z) for d in range(1, 4)]
    along = [device_at(core, x, (y + d) % 8, z) for d in range(1, 8)]
    above = [device_at(core, x, y, (z + d) % 8) for d in range(1, 8)]
    meet([across] + beside + along + above)

    at = pl.ds(pl.multiple_of(me * cells, cells), cells)
    first = send(term_ref.at[pl.ds((1 - core) * 4, 4)], crossed, sems.at[0, 0], sems.at[1, 0], across)
    first.start()
    runs = []
    for d in (2, 1, 3):
        runs.append(send(coarse_ref, run_ref.at[at], run_send.at[d - 1], run_recv.at[d - 1], others[d - 1]))
        runs[-1].start()
    own = pltpu.make_async_copy(coarse_ref, run_ref.at[at], local_sem)
    own.start()

    first.wait()
    for i in range(4):
        summed[i] = (term_ref[core * 4 + i].astype(F32) + crossed[i].astype(F32)).astype(BF)
    copies = []
    for d in range(1, 4):
        copies.append(send(summed.at[(x + d) % 4], lines.at[d - 1], sems.at[0, d], sems.at[1, d], beside[d - 1]))
        copies[-1].start()
    for copy in copies:
        copy.wait()
    total = summed[x].astype(F32)
    for d in range(3):
        total = total + lines[d].astype(F32)
    mine[:WIDE] = total.astype(BF)
    mine[WIDE:] = jnp.zeros((64, LANES), BF)

    copies = []
    for d in range(1, 8):
        to = pl.ds(pl.multiple_of((y + d) % 8 * 32, 32), 32)
        copies.append(send(mine.at[to], planes.at[d - 1], sems.at[0, 3 + d], sems.at[1, 3 + d], along[d - 1]))
        copies[-1].start()
    for copy in copies:
        copy.wait()
    total = mine[pl.ds(pl.multiple_of(y * 32, 32), 32)].astype(F32)
    for d in range(7):
        total = total + planes[d].astype(F32)
    pieces[z] = total.astype(BF)
    copies = []
    for d in range(1, 8):
        copies.append(send(pieces.at[z], pieces.at[z], sems.at[0, 10 + d], sems.at[1, 10 + d], above[d - 1]))
        copies[-1].start()
    for copy in copies:
        copy.wait()
    total = pieces[0].astype(F32)
    for i in range(1, 8):
        total = total + pieces[i].astype(F32)

    row = pl.ds(pl.multiple_of(y * 32, 32), 32)
    column[row] = total.astype(BF)
    copies = []
    for d in range(1, 8):
        copies.append(send(column.at[row], column.at[row], sems.at[0, 17 + d], sems.at[1, 17 + d], along[d - 1]))
        copies[-1].start()
    for copy in copies:
        copy.wait()
    spot = core * 4 + x
    whole[spot] = column[:WIDE]
    copies = []
    for d in range(1, 4):
        copies.append(send(whole.at[spot], whole.at[spot], sems.at[0, 24 + d], sems.at[1, 24 + d], beside[d - 1]))
        copies[-1].start()
    passed = [send(whole.at[spot], whole.at[spot], sems.at[0, 28], sems.at[1, 28], across)]
    passed[-1].start()
    for d in range(1, 4):
        copies[d - 1].wait()
        here = core * 4 + (x - d + 4) % 4
        passed.append(send(whole.at[here], whole.at[here], sems.at[0, 28 + d], sems.at[1, 28 + d], across))
        passed[-1].start()
    for copy in passed:
        copy.wait()
    for c in range(PARENT):
        grad_ref[c * WIDTH : (c + 1) * WIDTH, :] = jnp.transpose(whole[c].astype(F32))[:WIDTH] * (
            1.0 / math.sqrt(lax.axis_size("slab") * run_ref.shape[0])
        )
    own.wait()
    for run in runs:
        run.wait()


def params(**more):
    return pltpu.CompilerParams(vmem_limit_bytes=VMEM_LIMIT, **more)


def full(shape):
    return pl.BlockSpec(shape, lambda i: (0,) * len(shape))


def compute_first(points, live, gains, wq, wo, wi, wb):
    rows = points.shape[0]
    chunks, blocks = rows // CHUNK, rows // LANES
    return pl.pallas_call(
        first_kernel,
        grid=(chunks,),
        in_specs=[
            pl.BlockSpec((CHUNK, WIDTH), lambda i: (i, 0)),
            pl.BlockSpec((1, 4, LANES), lambda i: (i, 0, 0)),
            full(gains.shape), full(wq.shape), full(wo.shape), full(wi.shape), full(wb.shape),
        ],
        out_specs=[
            pl.BlockSpec((1, WIDTH, CHUNK), lambda i: (i, 0, 0)),
            pl.BlockSpec((4, 4, 32, WIDTH), lambda i: (0, i, 0, 0)),
        ],
        out_shape=[
            jax.ShapeDtypeStruct((chunks, WIDTH, CHUNK), F32),
            jax.ShapeDtypeStruct((4, blocks, 32, WIDTH), BF),
        ],
        scratch_shapes=[pltpu.VMEM(w.shape[::-1], BF) for w in (wq, wo, wi, wb)],
        compiler_params=params(),
    )(points, live, gains, wq, wo, wi, wb)


def compute_second(got, live, wq):
    blocks = got.shape[1]
    return pl.pallas_call(
        second_kernel,
        grid=(blocks // 4,),
        in_specs=[
            pl.BlockSpec((4, 4, 32, WIDTH), lambda i: (0, i, 0, 0)),
            pl.BlockSpec((1, 4, LANES), lambda i: (i, 0, 0)),
            full(wq.shape),
        ],
        out_specs=pl.BlockSpec((4, 4, 32, WIDTH), lambda i: (0, i, 0, 0)),
        out_shape=jax.ShapeDtypeStruct(got.shape, BF),
        scratch_shapes=[pltpu.VMEM(wq.shape[::-1], BF)],
        compiler_params=params(),
    )(got, live, wq)


def compute_third(state, heads, live, gains, wo, wi, wb):
    chunks = state.shape[0]
    return pl.pallas_call(
        third_kernel,
        grid=(chunks,),
        in_specs=[
            pl.BlockSpec((1, WIDTH, CHUNK), lambda i: (i, 0, 0)),
            pl.BlockSpec((4, 4, 32, WIDTH), lambda i: (0, i, 0, 0)),
            pl.BlockSpec((1, 4, LANES), lambda i: (i, 0, 0)),
            full(gains.shape), full(wo.shape), full(wi.shape), full(wb.shape),
        ],
        out_specs=pl.BlockSpec((CHUNK // PARENT, PARENT * LANES), lambda i: (i, 0)),
        out_shape=jax.ShapeDtypeStruct((chunks * CHUNK // PARENT, PARENT * LANES), BF),
        scratch_shapes=[pltpu.VMEM(w.shape[::-1], BF) for w in (wo, wi, wb)],
        compiler_params=params(),
    )(state, heads, live, gains, wo, wi, wb)


def compute_fourth(pooled, weight, gain, cot, live8):
    cells = pooled.shape[0]
    return pl.pallas_call(
        fourth_kernel,
        out_shape=[
            jax.ShapeDtypeStruct((cells, WIDE), BF),
            jax.ShapeDtypeStruct((cells * PARENT, WIDTH), BF),
            jax.ShapeDtypeStruct((PARENT, WIDE, LANES), BF),
        ],
        scratch_shapes=[pltpu.VMEM((PARENT * LANES, WIDE), BF), pltpu.VMEM((cells * PARENT, LANES), F32)],
        compiler_params=params(),
    )(pooled, weight, gain, cot, live8)


def deal_out(arr, number):
    return pl.pallas_call(
        deal_kernel,
        in_specs=[pl.BlockSpec(memory_space=pl.ANY)],
        out_specs=pl.BlockSpec(memory_space=pl.ANY),
        out_shape=jax.ShapeDtypeStruct(arr.shape, arr.dtype),
        scratch_shapes=[pltpu.SemaphoreType.DMA, pltpu.SemaphoreType.DMA((3,)), pltpu.SemaphoreType.DMA((3,))],
        compiler_params=pltpu.CompilerParams(collective_id=number, has_side_effects=True, vmem_limit_bytes=VMEM_LIMIT),
    )(arr)


def share(coarse, term):
    cells = coarse.shape[0]
    return pl.pallas_call(
        share_kernel,
        in_specs=[pl.BlockSpec(memory_space=pltpu.VMEM)] * 2,
        out_specs=[pl.BlockSpec(memory_space=pltpu.VMEM)] * 2,
        out_shape=[
            jax.ShapeDtypeStruct((4 * cells, WIDE), BF),
            jax.ShapeDtypeStruct((PARENT * WIDTH, WIDE), F32),
        ],
        scratch_shapes=[
            pltpu.VMEM((8, LANES), F32),
            pltpu.VMEM((4, WIDE, LANES), BF),
            pltpu.VMEM((4, WIDE, LANES), BF),
            pltpu.VMEM((3, WIDE, LANES), BF),
            pltpu.VMEM((256, LANES), BF),
            pltpu.VMEM((7, 32, LANES), BF),
            pltpu.VMEM((8, 32, LANES), BF),
            pltpu.VMEM((256, LANES), BF),
            pltpu.VMEM((8, LANES), F32),
            pltpu.VMEM((8, WIDE, LANES), BF),
            pltpu.SemaphoreType.DMA,
            pltpu.SemaphoreType.DMA((3,)),
            pltpu.SemaphoreType.DMA((3,)),
            pltpu.SemaphoreType.DMA((2, 32)),
        ],
        compiler_params=pltpu.CompilerParams(collective_id=3, has_side_effects=True, vmem_limit_bytes=VMEM_LIMIT),
    )(coarse, term)


def local(points, slot_mask, window_counts, block_gains, qkv_weight, out_weight, mlp_in, mlp_out, down_weight,
          coarse_gain, coarse_grad):
    rows = points.shape[2]
    blocks, cells = rows // LANES, rows // PARENT
    member = lax.axis_index("grp")
    points = points.reshape(rows, WIDTH)
    window = jnp.arange(rows, dtype=jnp.int32) // WINDOW
    live = jnp.where(window < window_counts.reshape(()), slot_mask.reshape(rows), 0)
    lanes = live.reshape(blocks, 4, 4, 2, 4).transpose(0, 4, 1, 3, 2).reshape(blocks, LANES)
    everyone = lax.all_gather(lanes.astype(BF), "grp").astype(F32)
    mine = lax.dynamic_slice_in_dim(everyone, member * 32, 32, 2)
    dealt = mine.transpose(1, 0, 2).reshape(blocks // 4, 4, LANES)
    lanes = lanes.astype(F32).reshape(blocks // 4, 4, LANES)
    gains = block_gains.reshape(4, WIDTH).T
    state, normed = compute_first(points, lanes, gains, qkv_weight[0], out_weight[0], mlp_in[0], mlp_out[0])
    got = deal_out(normed, 1)
    heads = compute_second(got, dealt, qkv_weight[1])
    back = deal_out(heads, 2)
    pooled = compute_third(state, back, lanes, gains, out_weight[1], mlp_in[1], mlp_out[1])
    cot = lax.dynamic_slice_in_dim(coarse_grad.reshape(4 * cells, WIDE), member * cells, cells, 0)
    coarse, fine, term = compute_fourth(
        pooled, down_weight, coarse_gain.reshape(1, WIDE), cot, live.reshape(cells, PARENT).astype(F32)
    )
    run, grad = share(coarse, term)
    return run.reshape(1, 4 * cells, WIDE), fine.reshape(1, 1, rows, WIDTH), grad


def solution(mesh):
    placed = (
        P("slab", "grp", None, None), P("slab", "grp", None), P("slab", "grp"), P(), P(), P(), P(), P(), P(), P(),
        P("slab", None, None),
    )
    return jax.shard_map(
        local,
        mesh=mesh,
        in_specs=placed,
        out_specs=(P("slab", None, None), P("slab", "grp", None, None), P()),
        check_vma=False,
    )
```

```python
import functools
import math

import jax
import jax.numpy as jnp
from jax import lax
from jax.experimental import pallas as pl
from jax.experimental.pallas import tpu as pltpu
from jax.sharding import PartitionSpec as P

MESH = pl.DeviceIdType.MESH
F32 = jnp.float32
BF = jnp.bfloat16
HEADS = 6
DEPTH = 16
WIDTH = 96
WINDOW = 32
LANES = 128
CHUNK = 512
PARENT = 8
WIDE = 192
EPS = 1e-05
NEG = -1e30
VMEM_LIMIT = 56 * 1024 * 1024


def dot(a, b, ca, cb):
    return lax.dot_general(a, b, (((ca,), (cb,)), ((), ())), preferred_element_type=F32)


def iota(shape, dim):
    return lax.broadcasted_iota(jnp.int32, shape, dim)


def place_of(slot):
    window, cell, odd, member = slot // 32, (slot % 32) // 8, (slot % 8) // 4, slot % 4
    return window * 32 + member * 8 + odd * 4 + cell


def onehot(rows, cols, match):
    return jnp.where(match(iota((rows, cols), 0), iota((rows, cols), 1)), 1.0, 0.0).astype(BF)


def deal_matrix():
    return onehot(LANES, LANES, lambda s, l: place_of(s) == l)


def cell_matrix():
    def match(r, l):
        child, cell = r // 16, r % 16
        return place_of((cell // 4) * 32 + (cell % 4) * 8 + child) == l

    return onehot(LANES, LANES, match)


def norm_rows(value, gain):
    mean = jnp.mean(value, axis=0, keepdims=True)
    centered = value - mean
    spread = jnp.mean(centered * centered, axis=0, keepdims=True)
    return centered * lax.rsqrt(spread + EPS) * gain


def gelu(x):
    return 0.5 * x * (1.0 + lax.erf(x * (0.5**0.5)))


def swap_matrix():
    def match(a, b):
        return (a // 128 * 32 + a // 32 % 4 * 8 + a // 8 % 4 * 128 + a % 8) == b

    return onehot(CHUNK, CHUNK, match)


def key_mask(live_row):
    own = iota((WINDOW, LANES), 1) % WINDOW == iota((WINDOW, LANES), 0)
    spread = jnp.where(own, jnp.broadcast_to(live_row, (WINDOW, LANES)), 0.0).astype(BF)
    same = onehot(LANES, LANES, lambda a, b: a // WINDOW == b // WINDOW)
    return (dot(spread, same, 1, 0) > 0.5) | own


def attend(qkv_t, live):
    which = (iota((1, 2 * LANES), 1) % LANES) // WINDOW
    none = jnp.zeros((DEPTH, LANES), BF)
    zero = jnp.zeros((), BF)
    parts = [qkv_t[:, b * LANES : (b + 1) * LANES] for b in range(4)]
    keys = [jnp.transpose(p[WIDTH : 2 * WIDTH].astype(F32)).astype(BF) for p in parts]
    masks = [key_mask(live[b : b + 1]) for b in range(4)]
    scores, spreads = {}, {}
    for b in range(4):
        for pair in range(HEADS // 2):
            cols = []
            for h in (2 * pair, 2 * pair + 1):
                q = parts[b][h * DEPTH : (h + 1) * DEPTH]
                cols.append(jnp.concatenate([q if i == h else none for i in range(HEADS)], 0))
            scores[b, pair] = dot(keys[b], jnp.concatenate(cols, 1), 1, 0)
    for at, score in scores.items():
        s = score.reshape(4, WINDOW, 2 * LANES)
        folded = jnp.where(which == 0, s[0], jnp.where(which == 1, s[1], jnp.where(which == 2, s[2], s[3])))
        mask = masks[at[0]]
        folded = jnp.where(jnp.concatenate([mask, mask], 1), folded, NEG)
        expo = jnp.exp(folded - jnp.max(folded, axis=0, keepdims=True))
        scale = 1.0 / jnp.sum(expo, axis=0, keepdims=True)
        half = expo.astype(BF)
        spreads[at] = jnp.concatenate([jnp.where(which == w, half, zero) for w in range(4)], 0), scale
    outs = []
    for b in range(4):
        rows = []
        for pair in range(HEADS // 2):
            spread, scale = spreads[b, pair]
            first = 2 * WIDTH + pair * 2 * DEPTH
            mixed = dot(parts[b][first : first + 2 * DEPTH], spread, 1, 0) * scale
            rows += [mixed[:DEPTH, :LANES], mixed[DEPTH:, LANES:]]
        outs.append(jnp.concatenate(rows, 0).astype(BF))
    return jnp.concatenate(outs, 1)


def project(w_t, normed):
    qkv = dot(w_t, normed, 1, 0)
    return jnp.concatenate([qkv[:WIDTH] * (DEPTH**-0.5), qkv[WIDTH:]], 0).astype(BF)


def feed_forward(state, gain, w_in_t, w_back_t):
    inner = norm_rows(state, gain).astype(BF)
    parts = [dot(w_in_t, inner[:, h * 256 : (h + 1) * 256], 1, 0) for h in range(2)]
    backs = [dot(w_back_t, gelu(p).astype(BF), 1, 0) for p in parts]
    return state + jnp.concatenate(backs, 1)


def turn(w):
    return jnp.transpose(w.astype(F32)).astype(BF)


def axis_ids():
    slab, grp = lax.axis_index("slab"), lax.axis_index("grp")
    core, x, z_lo, y = slab % 2, (slab // 2) % 4, (slab // 8) % 2, slab // 16
    return core, x, y, grp * 2 + z_lo


def device_at(core, x, y, z):
    return {"slab": ((y * 2 + z % 2) * 4 + x) * 2 + core, "grp": z // 2}


def send(src, dst, send_sem, recv_sem, peer):
    return pltpu.make_async_remote_copy(
        src_ref=src, dst_ref=dst, send_sem=send_sem, recv_sem=recv_sem, device_id=peer, device_id_type=MESH
    )


def whole_kernel(
    points_ref, mask_ref, count_ref, gains_ref, qkv_ref, out_ref, in_ref, back_ref, weight_ref, gain_ref, cot_ref,
    run_ref, fine_ref, grad_ref,
    wq, wo, wi, wb, gains, swap, wide, states, lives, lived, dealt, there, got, answer, heard, pooled, cot, spare,
    packed, runs, term, crossed, summed, lines, mine, planes, pieces, column, whole,
    cot_sem, live_sems, there_sems, answer_sems, run_sems, sems,
):
    core, x, y, z = axis_ids()
    me = lax.axis_index("grp")
    slab = lax.axis_index("slab")
    chunks, cells = states.shape[0], pooled.shape[0]
    group = [{"slab": slab, "grp": (me + d) % 4} for d in (1, 2, 3)]
    across = device_at(1 - core, x, y, z)
    beside = [device_at(core, (x + d) % 4, y, z) for d in range(1, 4)]
    along = [device_at(core, x, (y + d) % 8, z) for d in range(1, 8)]
    above = [device_at(core, x, y, (z + d) % 8) for d in range(1, 8)]
    barrier = pltpu.get_barrier_semaphore()
    peers = [across] + beside + along + above
    for peer in peers:
        pl.semaphore_signal(barrier, inc=1, device_id=peer, device_id_type=MESH)

    fetch = pltpu.make_async_copy(cot_ref.at[pl.ds(pl.multiple_of(me * cells, cells), cells)], cot, cot_sem)
    fetch.start()

    for b in range(2):
        wq[b] = turn(qkv_ref[b])
        wo[b] = turn(out_ref[b])
        wi[b] = turn(in_ref[b])
        wb[b] = turn(back_ref[b])
    gains[...] = jnp.transpose(jnp.concatenate([gains_ref[...], gains_ref[...]], 0))
    swap[...] = swap_matrix()
    for c in range(PARENT):
        wide[c * LANES : c * LANES + WIDTH, :] = weight_ref[c * WIDTH : (c + 1) * WIDTH, :]
        wide[c * LANES + WIDTH : (c + 1) * LANES, :] = jnp.zeros((LANES - WIDTH, WIDE), BF)
    blocks = mask_ref.shape[0]
    window = iota((blocks, LANES), 0) * 4 + iota((blocks, LANES), 1) // WINDOW
    live = jnp.where(window < count_ref[...], mask_ref[...].astype(F32), 0.0)
    live = dot(live.astype(BF), deal_matrix(), 1, 0)
    lived[me] = live
    for i in range(chunks):
        lives[i] = live[i * 4 : (i + 1) * 4]

    def live_copies():
        return [
            send(lived.at[me], lived.at[me], live_sems.at[0, d - 1], live_sems.at[1, d - 1], group[d - 1])
            for d in (2, 1, 3)
        ]

    def copies(i, src, dst, table):
        return [
            send(src.at[i, (me + d) % 4], dst.at[i, me], table.at[0, i, d - 1], table.at[1, i, d - 1], group[d - 1])
            for d in (2, 1, 3)
        ]

    def part(i, src, dst, table, rows):
        rows = dot(rows, swap[...], 1, 0).astype(BF)
        for r in range(4):
            src[i, r] = rows[:, r * LANES : (r + 1) * LANES]
        dst[i, me] = src[i, me]
        for copy in copies(i, src, dst, table):
            copy.start()

    def join(i, src, dst, table):
        for copy in copies(i, src, dst, table):
            copy.wait_recv()
        return dot(jnp.concatenate([dst[i, g] for g in range(4)], 1), swap[...], 1, 1).astype(BF)

    @pl.loop(0, chunks)
    def _(i):
        deal = deal_matrix()
        rows = points_ref[pl.ds(pl.multiple_of(i * CHUNK, CHUNK), CHUNK), :]
        state = jnp.concatenate([dot(rows[b * LANES : (b + 1) * LANES], deal, 0, 0) for b in range(4)], 1)
        qkv = project(wq[0], norm_rows(state, gains[:, 0:1]).astype(BF))
        state = state + dot(wo[0], attend(qkv, lives[i]), 1, 0)
        state = feed_forward(state, gains[:, 1:2], wi[0], wb[0])
        states[i] = state
        normed = norm_rows(state, gains[:, 2:3]).astype(BF)

        @pl.when(i == 0)
        def _():
            pl.semaphore_wait(barrier, len(peers))
            for copy in live_copies():
                copy.start()

        part(i, there, got, there_sems, normed)

    for copy in live_copies():
        copy.wait()
    total = jnp.zeros((blocks, LANES), F32)
    for g in range(4):
        pick = onehot(
            LANES,
            LANES,
            lambda a, b: (a // 32 == b // 32) & (a % 32 == me * 8 + b % 8) & (b % 32 // 8 == g),
        )
        total = total + dot(lived[g].astype(BF), pick, 1, 0)
    for i in range(chunks):
        dealt[i] = total[i * 4 : (i + 1) * 4]

    @pl.loop(0, chunks)
    def _(i):
        qkv = project(wq[1], join(i, there, got, there_sems))
        part(i, answer, heard, answer_sems, attend(qkv, dealt[i]))

    @pl.loop(0, chunks)
    def _(i):
        state = states[i] + dot(wo[1], join(i, answer, heard, answer_sems), 1, 0)
        state = feed_forward(state, gains[:, 3:4], wi[1], wb[1])
        deal = cell_matrix()
        row = lives[i]
        for b in range(4):
            fine = state[:, b * LANES : (b + 1) * LANES].astype(BF).astype(F32)
            fine = jnp.concatenate([fine, jnp.ones((16, LANES), F32)], 0) * row[b : b + 1]
            cell = dot(deal, fine.astype(BF), 1, 1).astype(BF)
            zero = jnp.zeros((16, LANES - WIDTH - 16), BF)
            at = pl.ds(pl.multiple_of(i * (CHUNK // PARENT) + b * 16, 16), 16)
            for c in range(PARENT):
                pooled[at, c * LANES : (c + 1) * LANES] = jnp.concatenate([cell[c * 16 : (c + 1) * 16], zero], 1)

    fetch.wait()
    every = pooled[...]
    weight = wide[...]
    gain = gain_ref[...]
    pre = dot(every, weight, 1, 0)
    centered = pre - jnp.mean(pre, -1, keepdims=True)
    scale = lax.rsqrt(jnp.mean(centered * centered, -1, keepdims=True) + EPS)
    unit = centered * scale
    slope = cot[...].astype(F32) * gain
    slope = slope - jnp.mean(slope, -1, keepdims=True) - unit * jnp.mean(slope * unit, -1, keepdims=True)
    half = (slope * scale).astype(BF)
    half_t = jnp.transpose(half.astype(F32)).astype(BF)
    order = [(1 - core) * 4, core * 4]
    for c in range(PARENT):
        term[c] = dot(half_t, every[:, c * LANES : (c + 1) * LANES], 1, 0).astype(BF)
    first = send(term.at[pl.ds(order[0], 4)], crossed, sems.at[0, 0], sems.at[1, 0], across)
    first.start()

    coarse = (unit * gain).astype(BF)
    run_ref[pl.ds(pl.multiple_of(me * cells, cells), cells), :] = coarse
    packed[:cells] = coarse[:, :LANES]
    tail = coarse[:, LANES:]
    packed[cells:] = jnp.concatenate([tail[: cells // 2], tail[cells // 2 :]], 1)
    shares = []
    for d in (2, 1, 3):
        shares.append(send(packed, runs.at[me], run_sems.at[0, d - 1], run_sems.at[1, d - 1], group[d - 1]))
        shares[-1].start()

    first.wait()
    for i in range(4):
        summed[i] = (term[order[1] + i].astype(F32) + crossed[i].astype(F32)).astype(BF)
    moves = []
    for d in range(1, 4):
        moves.append(send(summed.at[(x + d) % 4], lines.at[d - 1], sems.at[0, d], sems.at[1, d], beside[d - 1]))
        moves[-1].start()

    back = dot(half, weight, 1, 1)
    for c in range(PARENT):
        seen = every[:, c * LANES + WIDTH : c * LANES + WIDTH + 1].astype(F32)
        spare[pl.ds(c, cells, stride=PARENT), :] = back[:, c * LANES : (c + 1) * LANES] * seen

    for move in moves:
        move.wait()
    total = summed[x].astype(F32)
    for d in range(3):
        total = total + lines[d].astype(F32)
    mine[:WIDE] = total.astype(BF)
    mine[WIDE:] = jnp.zeros((256 - WIDE, LANES), BF)
    moves = []
    for d in range(1, 8):
        to = pl.ds(pl.multiple_of((y + d) % 8 * 32, 32), 32)
        moves.append(send(mine.at[to], planes.at[d - 1], sems.at[0, 3 + d], sems.at[1, 3 + d], along[d - 1]))
        moves[-1].start()
    fine_ref[...] = spare[:, :WIDTH].astype(BF)
    for move in moves:
        move.wait()
    row = pl.ds(pl.multiple_of(y * 32, 32), 32)
    total = mine[row].astype(F32)
    for d in range(7):
        total = total + planes[d].astype(F32)
    pieces[z] = total.astype(BF)
    moves = []
    for d in range(1, 8):
        moves.append(send(pieces.at[z], pieces.at[z], sems.at[0, 10 + d], sems.at[1, 10 + d], above[d - 1]))
        moves[-1].start()
    for move in moves:
        move.wait()
    total = pieces[0].astype(F32)
    for i in range(1, 8):
        total = total + pieces[i].astype(F32)
    column[row] = total.astype(BF)
    moves = []
    for d in range(1, 8):
        moves.append(send(column.at[row], column.at[row], sems.at[0, 17 + d], sems.at[1, 17 + d], along[d - 1]))
        moves[-1].start()
    for move in moves:
        move.wait()
    spot = core * 4 + x
    whole[spot] = column[:WIDE]
    moves = []
    for d in range(1, 4):
        moves.append(send(whole.at[spot], whole.at[spot], sems.at[0, 24 + d], sems.at[1, 24 + d], beside[d - 1]))
        moves[-1].start()
    passed = [send(whole.at[spot], whole.at[spot], sems.at[0, 28], sems.at[1, 28], across)]
    passed[-1].start()

    for share in shares:
        share.wait()
    for d in range(1, 4):
        g = (me + d) % 4
        at = pl.multiple_of(g * cells, cells)
        tail = runs[g, cells:]
        run_ref[pl.ds(at, cells), :LANES] = runs[g, :cells]
        run_ref[pl.ds(at, cells // 2), LANES:] = tail[:, : WIDE - LANES]
        run_ref[pl.ds(at + cells // 2, cells // 2), LANES:] = tail[:, WIDE - LANES :]

    for d in range(1, 4):
        moves[d - 1].wait()
        here = core * 4 + (x - d + 4) % 4
        passed.append(send(whole.at[here], whole.at[here], sems.at[0, 28 + d], sems.at[1, 28 + d], across))
        passed[-1].start()
    for copy in passed:
        copy.wait()
    for c in range(PARENT):
        grad_ref[c * WIDTH : (c + 1) * WIDTH, :] = jnp.transpose(whole[c].astype(F32))[:WIDTH] * (
            1.0 / math.sqrt(lax.axis_size("slab") * run_ref.shape[0])
        )

    @pl.loop(0, chunks)
    def _(i):
        for copy in copies(i, there, got, there_sems) + copies(i, answer, heard, answer_sems):
            copy.wait_send()


def local(points, slot_mask, window_counts, block_gains, qkv_weight, out_weight, mlp_in, mlp_out, down_weight,
          coarse_gain, coarse_grad):
    rows = points.shape[2]
    blocks, cells, chunks = rows // LANES, rows // PARENT, rows // CHUNK
    vmem = pl.BlockSpec(memory_space=pltpu.VMEM)
    sems = pltpu.SemaphoreType.DMA
    run, fine, grad = pl.pallas_call(
        whole_kernel,
        in_specs=[vmem] * 10 + [pl.BlockSpec(memory_space=pl.ANY)],
        out_specs=[vmem] * 3,
        out_shape=[
            jax.ShapeDtypeStruct((4 * cells, WIDE), BF),
            jax.ShapeDtypeStruct((rows, WIDTH), BF),
            jax.ShapeDtypeStruct((PARENT * WIDTH, WIDE), F32),
        ],
        scratch_shapes=[
            pltpu.VMEM((2, 3 * WIDTH, WIDTH), BF),
            pltpu.VMEM((2, WIDTH, WIDTH), BF),
            pltpu.VMEM((2, 4 * WIDTH, WIDTH), BF),
            pltpu.VMEM((2, WIDTH, 4 * WIDTH), BF),
            pltpu.VMEM((WIDTH, 8), F32),
            pltpu.VMEM((CHUNK, CHUNK), BF),
            pltpu.VMEM((PARENT * LANES, WIDE), BF),
            pltpu.VMEM((chunks, WIDTH, CHUNK), F32),
            pltpu.VMEM((chunks, 4, LANES), F32),
            pltpu.VMEM((4, blocks, LANES), F32),
            pltpu.VMEM((chunks, 4, LANES), F32),
            pltpu.VMEM((chunks, 4, WIDTH, LANES), BF),
            pltpu.VMEM((chunks, 4, WIDTH, LANES), BF),
            pltpu.VMEM((chunks, 4, WIDTH, LANES), BF),
            pltpu.VMEM((chunks, 4, WIDTH, LANES), BF),
            pltpu.VMEM((cells, PARENT * LANES), BF),
            pltpu.VMEM((cells, WIDE), BF),
            pltpu.VMEM((rows, LANES), F32),
            pltpu.VMEM((cells // 2 * 3, LANES), BF),
            pltpu.VMEM((4, cells // 2 * 3, LANES), BF),
            pltpu.VMEM((PARENT, WIDE, LANES), BF),
            pltpu.VMEM((4, WIDE, LANES), BF),
            pltpu.VMEM((4, WIDE, LANES), BF),
            pltpu.VMEM((3, WIDE, LANES), BF),
            pltpu.VMEM((256, LANES), BF),
            pltpu.VMEM((7, 32, LANES), BF),
            pltpu.VMEM((8, 32, LANES), BF),
            pltpu.VMEM((256, LANES), BF),
            pltpu.VMEM((8, WIDE, LANES), BF),
            sems,
            sems((2, 3)),
            sems((2, chunks, 3)),
            sems((2, chunks, 3)),
            sems((2, 3)),
            sems((2, 32)),
        ],
        compiler_params=pltpu.CompilerParams(
            collective_id=1, has_side_effects=True, vmem_limit_bytes=VMEM_LIMIT
        ),
    )(
        points.reshape(rows, WIDTH), slot_mask.reshape(blocks, LANES), window_counts, block_gains.reshape(4, WIDTH),
        qkv_weight, out_weight, mlp_in, mlp_out, down_weight, coarse_gain.reshape(1, WIDE),
        coarse_grad.reshape(4 * cells, WIDE),
    )
    return run.reshape(1, 4 * cells, WIDE), fine.reshape(1, 1, rows, WIDTH), grad


def solution(mesh):
    placed = (
        P("slab", "grp", None, None), P("slab", "grp", None), P("slab", "grp"), P(), P(), P(), P(), P(), P(), P(),
        P("slab", None, None),
    )
    return jax.shard_map(
        local,
        mesh=mesh,
        in_specs=placed,
        out_specs=(P("slab", None, None), P("slab", "grp", None, None), P()),
        check_vma=False,
    )
```

```python
import functools
import math

import jax
import jax.numpy as jnp
from jax import lax
from jax.experimental import pallas as pl
from jax.experimental.pallas import tpu as pltpu
from jax.sharding import PartitionSpec as P

MESH = pl.DeviceIdType.MESH
F32 = jnp.float32
BF = jnp.bfloat16
HEADS = 6
DEPTH = 16
WIDTH = 96
WINDOW = 32
LANES = 128
CHUNK = 512
PARENT = 8
WIDE = 192
EPS = 1e-05
NEG = -1e30
VMEM_LIMIT = 56 * 1024 * 1024


def dot(a, b, ca, cb):
    return lax.dot_general(a, b, (((ca,), (cb,)), ((), ())), preferred_element_type=F32)


def iota(shape, dim):
    return lax.broadcasted_iota(jnp.int32, shape, dim)


def onehot(rows, cols, match):
    return jnp.where(match(iota((rows, cols), 0), iota((rows, cols), 1)), 1.0, 0.0).astype(BF)


def cell_matrix():
    return onehot(LANES, LANES, lambda r, l: r % 16 * PARENT + r // 16 == l)


def norm_rows(value, gain):
    mean = jnp.mean(value, axis=0, keepdims=True)
    centered = value - mean
    spread = jnp.mean(centered * centered, axis=0, keepdims=True)
    return centered * lax.rsqrt(spread + EPS) * gain


def gelu(x):
    return 0.5 * x * (1.0 + lax.erf(x * (0.5**0.5)))


def swap_matrix():
    def match(a, b):
        return a % 4 * LANES + a // WINDOW * 8 + a % WINDOW // 4 == b

    return onehot(CHUNK, CHUNK, match)


def key_mask(live_row):
    own = iota((WINDOW, LANES), 1) % WINDOW == iota((WINDOW, LANES), 0)
    spread = jnp.where(own, jnp.broadcast_to(live_row, (WINDOW, LANES)), 0.0).astype(BF)
    same = onehot(LANES, LANES, lambda a, b: a // WINDOW == b // WINDOW)
    return (dot(spread, same, 1, 0) > 0.5) | own


def attend(qkv_t, live):
    which = (iota((1, 2 * LANES), 1) % LANES) // WINDOW
    none = jnp.zeros((DEPTH, LANES), BF)
    zero = jnp.zeros((), BF)
    parts = [qkv_t[:, b * LANES : (b + 1) * LANES] for b in range(4)]
    keys = [jnp.transpose(p[WIDTH : 2 * WIDTH].astype(F32)).astype(BF) for p in parts]
    masks = [key_mask(live[b : b + 1]) for b in range(4)]
    scores, spreads = {}, {}
    for b in range(4):
        for pair in range(HEADS // 2):
            cols = []
            for h in (2 * pair, 2 * pair + 1):
                q = parts[b][h * DEPTH : (h + 1) * DEPTH]
                cols.append(jnp.concatenate([q if i == h else none for i in range(HEADS)], 0))
            scores[b, pair] = dot(keys[b], jnp.concatenate(cols, 1), 1, 0)
    for at, score in scores.items():
        s = score.reshape(4, WINDOW, 2 * LANES)
        folded = jnp.where(which == 0, s[0], jnp.where(which == 1, s[1], jnp.where(which == 2, s[2], s[3])))
        mask = masks[at[0]]
        folded = jnp.where(jnp.concatenate([mask, mask], 1), folded, NEG)
        expo = jnp.exp(folded - jnp.max(folded, axis=0, keepdims=True))
        scale = 1.0 / jnp.sum(expo, axis=0, keepdims=True)
        half = expo.astype(BF)
        spreads[at] = jnp.concatenate([jnp.where(which == w, half, zero) for w in range(4)], 0), scale
    outs = []
    for b in range(4):
        rows = []
        for pair in range(HEADS // 2):
            spread, scale = spreads[b, pair]
            first = 2 * WIDTH + pair * 2 * DEPTH
            mixed = dot(parts[b][first : first + 2 * DEPTH], spread, 1, 0) * scale
            rows += [mixed[:DEPTH, :LANES], mixed[DEPTH:, LANES:]]
        outs.append(jnp.concatenate(rows, 0).astype(BF))
    return jnp.concatenate(outs, 1)


def project(w_t, normed):
    qkv = dot(w_t, normed, 1, 0)
    return jnp.concatenate([qkv[:WIDTH] * (DEPTH**-0.5), qkv[WIDTH:]], 0).astype(BF)


def feed_forward(state, gain, w_in_t, w_back_t):
    inner = norm_rows(state, gain).astype(BF)
    parts = [dot(w_in_t, inner[:, h * 256 : (h + 1) * 256], 1, 0) for h in range(2)]
    backs = [dot(w_back_t, gelu(p).astype(BF), 1, 0) for p in parts]
    return state + jnp.concatenate(backs, 1)


def turn(w):
    return jnp.transpose(w.astype(F32)).astype(BF)


def axis_ids():
    slab, grp = lax.axis_index("slab"), lax.axis_index("grp")
    core, x, z_lo, y = slab % 2, (slab // 2) % 4, (slab // 8) % 2, slab // 16
    return core, x, y, grp * 2 + z_lo


def device_at(core, x, y, z):
    return {"slab": ((y * 2 + z % 2) * 4 + x) * 2 + core, "grp": z // 2}


def send(src, dst, send_sem, recv_sem, peer):
    return pltpu.make_async_remote_copy(
        src_ref=src, dst_ref=dst, send_sem=send_sem, recv_sem=recv_sem, device_id=peer, device_id_type=MESH
    )


def whole_kernel(
    points_ref, mask_ref, count_ref, gains_ref, qkv_ref, out_ref, in_ref, back_ref, weight_ref, gain_ref, cot_ref,
    run_ref, fine_ref, grad_ref,
    wq, wo, wi, gains, gain, swap, wide, states, lives, lived, dealt, there, got, answer, heard, pooled, cot, term,
    crossed, summed, lines, mine, planes, pieces, column, whole,
    cot_sem, live_sems, there_sems, answer_sems, run_sems, sems,
):
    core, x, y, z = axis_ids()
    me = lax.axis_index("grp")
    slab = lax.axis_index("slab")
    chunks, cells = states.shape[0], pooled.shape[0]
    group = [{"slab": slab, "grp": (me + d) % 4} for d in (1, 2, 3)]
    across = device_at(1 - core, x, y, z)
    beside = [device_at(core, (x + d) % 4, y, z) for d in range(1, 4)]
    along = [device_at(core, x, (y + d) % 8, z) for d in range(1, 8)]
    above = [device_at(core, x, y, (z + d) % 8) for d in range(1, 8)]
    barrier = pltpu.get_barrier_semaphore()
    peers = [across] + beside + along + above
    for peer in peers:
        pl.semaphore_signal(barrier, inc=1, device_id=peer, device_id_type=MESH)

    fetch = pltpu.make_async_copy(cot_ref.at[:, pl.ds(pl.multiple_of(me * cells, LANES), cells)], cot, cot_sem)
    fetch.start()

    for b in range(2):
        wq[b] = turn(qkv_ref[b])
        wo[b] = turn(out_ref[b])
        wi[b] = turn(in_ref[b])
    gains[...] = jnp.transpose(jnp.concatenate([gains_ref[...], gains_ref[...]], 0))
    gain[...] = jnp.transpose(jnp.broadcast_to(gain_ref[...], (8, WIDE)))
    swap[...] = swap_matrix()
    for c in range(PARENT):
        wide[:, c * LANES : (c + 1) * LANES] = jnp.concatenate(
            [weight_ref[:, c * WIDTH : (c + 1) * WIDTH], jnp.zeros((WIDE, LANES - WIDTH), BF)], 1
        )
    blocks = mask_ref.shape[0]
    window = iota((blocks, LANES), 0) * 4 + iota((blocks, LANES), 1) // WINDOW
    live = jnp.where(window < count_ref[...], mask_ref[...].astype(F32), 0.0)
    lived[me] = live
    for i in range(chunks):
        lives[i] = live[i * 4 : (i + 1) * 4]

    def live_copies():
        return [
            send(lived.at[me], lived.at[me], live_sems.at[0, d - 1], live_sems.at[1, d - 1], group[d - 1])
            for d in (2, 1, 3)
        ]

    def copies(i, src, dst, table):
        return [
            send(src.at[i, (me + d) % 4], dst.at[i, me], table.at[0, i, d - 1], table.at[1, i, d - 1], group[d - 1])
            for d in (2, 1, 3)
        ]

    def part(i, src, dst, table, rows):
        rows = dot(rows, swap[...], 1, 0).astype(BF)
        for r in range(4):
            src[i, r] = rows[:, r * LANES : (r + 1) * LANES]
        dst[i, me] = src[i, me]
        for copy in copies(i, src, dst, table):
            copy.start()

    def join(i, src, dst, table):
        for copy in copies(i, src, dst, table):
            copy.wait_recv()
        return dot(jnp.concatenate([dst[i, g] for g in range(4)], 1), swap[...], 1, 1).astype(BF)

    @pl.loop(0, chunks)
    def _(i):
        state = points_ref[:, pl.ds(pl.multiple_of(i * CHUNK, CHUNK), CHUNK)].astype(F32)
        qkv = project(wq[0], norm_rows(state, gains[:, 0:1]).astype(BF))
        state = state + dot(wo[0], attend(qkv, lives[i]), 1, 0)
        state = feed_forward(state, gains[:, 1:2], wi[0], back_ref[0])
        states[i] = state
        normed = norm_rows(state, gains[:, 2:3]).astype(BF)

        @pl.when(i == 0)
        def _():
            pl.semaphore_wait(barrier, len(peers))
            for copy in live_copies():
                copy.start()

        part(i, there, got, there_sems, normed)

    for copy in live_copies():
        copy.wait()
    total = jnp.zeros((blocks, LANES), F32)
    for g in range(4):
        pick = onehot(
            LANES,
            LANES,
            lambda a, b: (b % 4 == g) & (a == b - g + me),
        )
        total = total + dot(lived[g].astype(BF), pick, 1, 0)
    for i in range(chunks):
        dealt[i] = total[i * 4 : (i + 1) * 4]

    @pl.loop(0, chunks)
    def _(i):
        qkv = project(wq[1], join(i, there, got, there_sems))
        part(i, answer, heard, answer_sems, attend(qkv, dealt[i]))

    @pl.loop(0, chunks)
    def _(i):
        state = states[i] + dot(wo[1], join(i, answer, heard, answer_sems), 1, 0)
        state = feed_forward(state, gains[:, 3:4], wi[1], back_ref[1])
        deal = cell_matrix()
        row = lives[i]
        for b in range(4):
            fine = state[:, b * LANES : (b + 1) * LANES].astype(BF).astype(F32) * row[b : b + 1]
            fine = jnp.concatenate([fine.astype(BF), jnp.zeros((LANES - WIDTH, LANES), BF)], 0)
            cell = dot(deal, fine, 1, 1).astype(BF)
            at = pl.ds(pl.multiple_of(i * (CHUNK // PARENT) + b * 16, 16), 16)
            for c in range(PARENT):
                pooled[at, c * LANES : (c + 1) * LANES] = cell[c * 16 : (c + 1) * 16]

    fetch.wait()
    every = pooled[...]
    weight = wide[...]
    column_gain = gain[:, 0:1]
    pre = dot(weight, every, 1, 1)
    centered = pre - jnp.mean(pre, axis=0, keepdims=True)
    scale = lax.rsqrt(jnp.mean(centered * centered, axis=0, keepdims=True) + EPS)
    unit = centered * scale
    slope = cot[...].astype(F32) * column_gain
    slope = slope - jnp.mean(slope, axis=0, keepdims=True) - unit * jnp.mean(slope * unit, axis=0, keepdims=True)
    half = (slope * scale).astype(BF)
    order = [(1 - core) * 4, core * 4]
    for c in range(PARENT):
        term[c] = dot(half, every[:, c * LANES : (c + 1) * LANES], 1, 0).astype(BF)
    first = send(term.at[pl.ds(order[0], 4)], crossed, sems.at[0, 0], sems.at[1, 0], across)
    first.start()

    ours = pl.ds(pl.multiple_of(me * cells, LANES), cells)
    run_ref[:, ours] = (unit * column_gain).astype(BF)
    shares = []

    def share(pieces_now):
        for piece in pieces_now:
            lanes = pl.ds(pl.multiple_of(me * cells + piece // 2 * LANES, LANES), LANES)
            spot = run_ref.at[piece % 2 * WIDTH : piece % 2 * WIDTH + WIDTH, lanes]
            for d in (2, 1, 3):
                shares.append(
                    send(spot, spot, run_sems.at[0, piece, d - 1], run_sems.at[1, piece, d - 1], group[d - 1])
                )
                shares[-1].start()

    first.wait()
    for i in range(4):
        summed[i] = (term[order[1] + i].astype(F32) + crossed[i].astype(F32)).astype(BF)
    moves = []
    for d in range(1, 4):
        moves.append(send(summed.at[(x + d) % 4], lines.at[d - 1], sems.at[0, d], sems.at[1, d], beside[d - 1]))
        moves[-1].start()
    share((0,))

    back = dot(half, weight, 0, 0).astype(BF)
    deal = cell_matrix()
    for b in range(blocks):
        cell = jnp.concatenate(
            [back[b * 16 : (b + 1) * 16, c * LANES : (c + 1) * LANES] for c in range(PARENT)], 0
        )
        fine = dot(cell, deal, 0, 0)[:WIDTH] * lives[b // 4, b % 4 : b % 4 + 1]
        fine_ref[:, b * LANES : (b + 1) * LANES] = fine.astype(BF)

    for move in moves:
        move.wait()
    total = summed[x].astype(F32)
    for d in range(3):
        total = total + lines[d].astype(F32)
    mine[:WIDE] = total.astype(BF)
    mine[WIDE:] = jnp.zeros((256 - WIDE, LANES), BF)
    moves = []
    for d in range(1, 8):
        to = pl.ds(pl.multiple_of((y + d) % 8 * 32, 32), 32)
        moves.append(send(mine.at[to], planes.at[d - 1], sems.at[0, 3 + d], sems.at[1, 3 + d], along[d - 1]))
        moves[-1].start()
    share((1, 2))
    for move in moves:
        move.wait()
    row = pl.ds(pl.multiple_of(y * 32, 32), 32)
    total = mine[row].astype(F32)
    for d in range(7):
        total = total + planes[d].astype(F32)
    pieces[z] = total.astype(BF)
    moves = []
    for d in range(1, 8):
        moves.append(send(pieces.at[z], pieces.at[z], sems.at[0, 10 + d], sems.at[1, 10 + d], above[d - 1]))
        moves[-1].start()
    share((3,))
    for move in moves:
        move.wait()
    total = pieces[0].astype(F32)
    for i in range(1, 8):
        total = total + pieces[i].astype(F32)
    column[row] = total.astype(BF)
    moves = []
    for d in range(1, 8):
        moves.append(send(column.at[row], column.at[row], sems.at[0, 17 + d], sems.at[1, 17 + d], along[d - 1]))
        moves[-1].start()
    share((4, 5))
    for move in moves:
        move.wait()
    spot = core * 4 + x
    whole[spot] = column[:WIDE]
    moves = []
    for d in range(1, 4):
        moves.append(send(whole.at[spot], whole.at[spot], sems.at[0, 24 + d], sems.at[1, 24 + d], beside[d - 1]))
        moves[-1].start()
    passed = [send(whole.at[spot], whole.at[spot], sems.at[0, 28], sems.at[1, 28], across)]
    passed[-1].start()

    for d in range(1, 4):
        moves[d - 1].wait()
        here = core * 4 + (x - d + 4) % 4
        passed.append(send(whole.at[here], whole.at[here], sems.at[0, 28 + d], sems.at[1, 28 + d], across))
        passed[-1].start()
    for copy in passed:
        copy.wait()
    for c in range(PARENT):
        grad_ref[:, c * WIDTH : (c + 1) * WIDTH] = whole[c][:, :WIDTH].astype(F32) * (
            1.0 / math.sqrt(lax.axis_size("slab") * run_ref.shape[1])
        )
    for share in shares:
        share.wait()

    @pl.loop(0, chunks)
    def _(i):
        for copy in copies(i, there, got, there_sems) + copies(i, answer, heard, answer_sems):
            copy.wait_send()


def local(points, slot_mask, window_counts, block_gains, qkv_weight, out_weight, mlp_in, mlp_out, down_weight,
          coarse_gain, coarse_grad):
    rows = points.shape[2]
    blocks, cells, chunks = rows // LANES, rows // PARENT, rows // CHUNK
    vmem = pl.BlockSpec(memory_space=pltpu.VMEM)
    sems = pltpu.SemaphoreType.DMA
    run, fine, grad = pl.pallas_call(
        whole_kernel,
        in_specs=[vmem] * 10 + [pl.BlockSpec(memory_space=pl.ANY)],
        out_specs=[vmem] * 3,
        out_shape=[
            jax.ShapeDtypeStruct((WIDE, 4 * cells), BF),
            jax.ShapeDtypeStruct((WIDTH, rows), BF),
            jax.ShapeDtypeStruct((WIDE, PARENT * WIDTH), F32),
        ],
        scratch_shapes=[
            pltpu.VMEM((2, 3 * WIDTH, WIDTH), BF),
            pltpu.VMEM((2, WIDTH, WIDTH), BF),
            pltpu.VMEM((2, 4 * WIDTH, WIDTH), BF),
            pltpu.VMEM((WIDTH, 8), F32),
            pltpu.VMEM((WIDE, 8), F32),
            pltpu.VMEM((CHUNK, CHUNK), BF),
            pltpu.VMEM((WIDE, PARENT * LANES), BF),
            pltpu.VMEM((chunks, WIDTH, CHUNK), F32),
            pltpu.VMEM((chunks, 4, LANES), F32),
            pltpu.VMEM((4, blocks, LANES), F32),
            pltpu.VMEM((chunks, 4, LANES), F32),
            pltpu.VMEM((chunks, 4, WIDTH, LANES), BF),
            pltpu.VMEM((chunks, 4, WIDTH, LANES), BF),
            pltpu.VMEM((chunks, 4, WIDTH, LANES), BF),
            pltpu.VMEM((chunks, 4, WIDTH, LANES), BF),
            pltpu.VMEM((cells, PARENT * LANES), BF),
            pltpu.VMEM((WIDE, cells), BF),
            pltpu.VMEM((PARENT, WIDE, LANES), BF),
            pltpu.VMEM((4, WIDE, LANES), BF),
            pltpu.VMEM((4, WIDE, LANES), BF),
            pltpu.VMEM((3, WIDE, LANES), BF),
            pltpu.VMEM((256, LANES), BF),
            pltpu.VMEM((7, 32, LANES), BF),
            pltpu.VMEM((8, 32, LANES), BF),
            pltpu.VMEM((256, LANES), BF),
            pltpu.VMEM((8, WIDE, LANES), BF),
            sems,
            sems((2, 3)),
            sems((2, chunks, 3)),
            sems((2, chunks, 3)),
            sems((2, 6, 3)),
            sems((2, 32)),
        ],
        compiler_params=pltpu.CompilerParams(
            collective_id=1, has_side_effects=True, vmem_limit_bytes=VMEM_LIMIT
        ),
    )(
        points.reshape(rows, WIDTH).T, slot_mask.reshape(blocks, LANES), window_counts, block_gains.reshape(4, WIDTH),
        qkv_weight, out_weight, mlp_in, jnp.swapaxes(mlp_out, 1, 2), down_weight.T, coarse_gain.reshape(1, WIDE),
        coarse_grad.reshape(4 * cells, WIDE).T,
    )
    return run.T.reshape(1, 4 * cells, WIDE), fine.T.reshape(1, 1, rows, WIDTH), grad.T


def solution(mesh):
    placed = (
        P("slab", "grp", None, None), P("slab", "grp", None), P("slab", "grp"), P(), P(), P(), P(), P(), P(), P(),
        P("slab", None, None),
    )
    return jax.shard_map(
        local,
        mesh=mesh,
        in_specs=placed,
        out_specs=(P("slab", None, None), P("slab", "grp", None, None), P()),
        check_vma=False,
    )
```

```python
import functools
import math

import jax
import jax.numpy as jnp
from jax import lax
from jax.experimental import pallas as pl
from jax.experimental.pallas import tpu as pltpu
from jax.sharding import PartitionSpec as P

MESH = pl.DeviceIdType.MESH
F32 = jnp.float32
BF = jnp.bfloat16
HEADS = 6
DEPTH = 16
WIDTH = 96
WINDOW = 32
LANES = 128
CHUNK = 512
PARENT = 8
WIDE = 192
EPS = 1e-05
NEG = -1e30
VMEM_LIMIT = 56 * 1024 * 1024


def dot(a, b, ca, cb):
    return lax.dot_general(a, b, (((ca,), (cb,)), ((), ())), preferred_element_type=F32)


def iota(shape, dim):
    return lax.broadcasted_iota(jnp.int32, shape, dim)


def onehot(rows, cols, match):
    return jnp.where(match(iota((rows, cols), 0), iota((rows, cols), 1)), 1.0, 0.0).astype(BF)


def cell_matrix():
    return onehot(LANES, LANES, lambda r, l: r % 16 * PARENT + r // 16 == l)


def norm_rows(value, gain):
    mean = jnp.mean(value, axis=0, keepdims=True)
    centered = value - mean
    spread = jnp.mean(centered * centered, axis=0, keepdims=True)
    return centered * lax.rsqrt(spread + EPS) * gain


def gelu(x):
    return 0.5 * x * (1.0 + lax.erf(x * (0.5**0.5)))


def lane_of(slot):
    return slot % 4 * LANES + slot // WINDOW * 8 + slot % WINDOW // 4


def key_mask(live_row):
    own = iota((WINDOW, LANES), 1) % WINDOW == iota((WINDOW, LANES), 0)
    spread = jnp.where(own, jnp.broadcast_to(live_row, (WINDOW, LANES)), 0.0).astype(BF)
    same = onehot(LANES, LANES, lambda a, b: a // WINDOW == b // WINDOW)
    return (dot(spread, same, 1, 0) > 0.5) | own


def attend(qkv_t, live):
    which = (iota((1, 2 * LANES), 1) % LANES) // WINDOW
    none = jnp.zeros((DEPTH, LANES), BF)
    zero = jnp.zeros((), BF)
    parts = [qkv_t[:, b * LANES : (b + 1) * LANES] for b in range(len(live))]
    keys = [jnp.transpose(p[WIDTH : 2 * WIDTH].astype(F32)).astype(BF) for p in parts]
    masks = [key_mask(row) for row in live]
    scores, spreads = {}, {}
    for b in range(len(live)):
        for pair in range(HEADS // 2):
            cols = []
            for h in (2 * pair, 2 * pair + 1):
                q = parts[b][h * DEPTH : (h + 1) * DEPTH]
                cols.append(jnp.concatenate([q if i == h else none for i in range(HEADS)], 0))
            scores[b, pair] = dot(keys[b], jnp.concatenate(cols, 1), 1, 0)
    for at, score in scores.items():
        s = score.reshape(4, WINDOW, 2 * LANES)
        folded = jnp.where(which == 0, s[0], jnp.where(which == 1, s[1], jnp.where(which == 2, s[2], s[3])))
        mask = masks[at[0]]
        folded = jnp.where(jnp.concatenate([mask, mask], 1), folded, NEG)
        expo = jnp.exp(folded - jnp.max(folded, axis=0, keepdims=True))
        scale = 1.0 / jnp.sum(expo, axis=0, keepdims=True)
        half = expo.astype(BF)
        spreads[at] = jnp.concatenate([jnp.where(which == w, half, zero) for w in range(4)], 0), scale
    outs = []
    for b in range(len(live)):
        rows = []
        for pair in range(HEADS // 2):
            spread, scale = spreads[b, pair]
            first = 2 * WIDTH + pair * 2 * DEPTH
            mixed = dot(parts[b][first : first + 2 * DEPTH], spread, 1, 0) * scale
            rows += [mixed[:DEPTH, :LANES], mixed[DEPTH:, LANES:]]
        outs.append(jnp.concatenate(rows, 0).astype(BF))
    return jnp.concatenate(outs, 1)


def project(w_t, normed):
    qkv = dot(w_t, normed, 1, 0)
    return jnp.concatenate([qkv[:WIDTH] * (DEPTH**-0.5), qkv[WIDTH:]], 0).astype(BF)


def feed_forward(state, gain, w_in_t, w_back_t):
    inner = norm_rows(state, gain).astype(BF)
    parts = [dot(w_in_t, inner[:, at : at + 256], 1, 0) for at in range(0, state.shape[1], 256)]
    backs = [dot(w_back_t, gelu(p).astype(BF), 1, 0) for p in parts]
    return state + jnp.concatenate(backs, 1)


def turn(w):
    return jnp.transpose(w.astype(F32)).astype(BF)


def axis_ids():
    slab, grp = lax.axis_index("slab"), lax.axis_index("grp")
    core, x, z_lo, y = slab % 2, (slab // 2) % 4, (slab // 8) % 2, slab // 16
    return core, x, y, grp * 2 + z_lo


def device_at(core, x, y, z):
    return {"slab": ((y * 2 + z % 2) * 4 + x) * 2 + core, "grp": z // 2}


def send(src, dst, send_sem, recv_sem, peer):
    return pltpu.make_async_remote_copy(
        src_ref=src, dst_ref=dst, send_sem=send_sem, recv_sem=recv_sem, device_id=peer, device_id_type=MESH
    )


def whole_kernel(
    points_ref, mask_ref, count_ref, gains_ref, qkv_ref, out_ref, in_ref, back_ref, weight_ref, gain_ref, cot_ref,
    run_ref, fine_ref, grad_ref,
    wq, wo, wi, gains, gain, swap, wide, states, lives, lived, dealt, there, got, answer, heard, pooled, cot, loaded, term,
    crossed, summed, lines, mine, planes, pieces, column, whole,
    cot_sem, load_sem, live_sems, there_sems, answer_sems, run_sems, sems,
):
    core, x, y, z = axis_ids()
    me = lax.axis_index("grp")
    slab = lax.axis_index("slab")
    chunks, cells = there.shape[0], pooled.shape[0]
    group = [{"slab": slab, "grp": (me + d) % 4} for d in (1, 2, 3)]
    across = device_at(1 - core, x, y, z)
    beside = [device_at(core, (x + d) % 4, y, z) for d in range(1, 4)]
    along = [device_at(core, x, (y + d) % 8, z) for d in range(1, 8)]
    above = [device_at(core, x, y, (z + d) % 8) for d in range(1, 8)]
    barrier = pltpu.get_barrier_semaphore()
    peers = [across] + beside + along + above
    for peer in peers:
        pl.semaphore_signal(barrier, inc=1, device_id=peer, device_id_type=MESH)

    fetch = pltpu.make_async_copy(cot_ref.at[:, pl.ds(pl.multiple_of(me * cells, LANES), cells)], cot, cot_sem)
    fetch.start()

    load = pltpu.make_async_copy(weight_ref, loaded, load_sem)
    load.start()

    wq[0] = turn(qkv_ref[0])
    wo[0] = turn(out_ref[0])
    wi[0] = turn(in_ref[0])
    gains[...] = jnp.transpose(jnp.concatenate([gains_ref[...], gains_ref[...]], 0))
    gain[...] = jnp.transpose(jnp.broadcast_to(gain_ref[...], (8, WIDE)))
    swap[0] = onehot(CHUNK, CHUNK, lambda a, b: lane_of(a) == b)
    swap[1] = onehot(CHUNK, CHUNK, lambda a, b: lane_of(b) == a)
    blocks = mask_ref.shape[0]
    window = iota((blocks, LANES), 0) * 4 + iota((blocks, LANES), 1) // WINDOW
    live = jnp.where(window < count_ref[...], mask_ref[...].astype(F32), 0.0)
    lived[me] = live
    for i in range(chunks):
        lives[i] = live[i * 4 : (i + 1) * 4]

    def live_copies():
        return [
            send(lived.at[me], lived.at[me], live_sems.at[0, d - 1], live_sems.at[1, d - 1], group[d - 1])
            for d in (2, 1, 3)
        ]

    def copies(i, src, dst, table):
        return [
            send(src.at[i, (me + d) % 4], dst.at[i, me], table.at[0, i, d - 1], table.at[1, i, d - 1], group[d - 1])
            for d in (2, 1, 3)
        ]

    def part(pair, src, dst, table, rows):
        for i, half in ((2 * pair, rows[:, :CHUNK]), (2 * pair + 1, rows[:, CHUNK:])):
            half = dot(half, swap[0], 1, 0).astype(BF)
            for r in range(4):
                src[i, r] = half[:, r * LANES : (r + 1) * LANES]
            dst[i, me] = src[i, me]
            for copy in copies(i, src, dst, table):
                copy.start()

    def join(pair, src, dst, table):
        halves = []
        for i in (2 * pair, 2 * pair + 1):
            for copy in copies(i, src, dst, table):
                copy.wait_recv()
            halves.append(dot(jnp.concatenate([dst[i, g] for g in range(4)], 1), swap[1], 1, 0).astype(BF))
        return jnp.concatenate(halves, 1)

    def rows_of(table, pair):
        return [table[2 * pair + b // 4][b % 4 : b % 4 + 1] for b in range(8)]

    @pl.loop(0, chunks // 2)
    def _(i):
        state = points_ref[:, pl.ds(pl.multiple_of(i * 2 * CHUNK, CHUNK), 2 * CHUNK)].astype(F32)
        qkv = project(wq[0], norm_rows(state, gains[:, 0:1]).astype(BF))
        state = state + dot(wo[0], attend(qkv, rows_of(lives, i)), 1, 0)
        state = feed_forward(state, gains[:, 1:2], wi[0], back_ref[0])
        states[i] = state
        normed = norm_rows(state, gains[:, 2:3]).astype(BF)

        @pl.when(i == 0)
        def _():
            pl.semaphore_wait(barrier, len(peers))
            for copy in live_copies():
                copy.start()

        part(i, there, got, there_sems, normed)

    wq[1] = turn(qkv_ref[1])
    wo[1] = turn(out_ref[1])
    wi[1] = turn(in_ref[1])
    load.wait()
    for c in range(PARENT):
        wide[:, c * LANES : (c + 1) * LANES] = jnp.concatenate(
            [loaded[:, c * WIDTH : (c + 1) * WIDTH], jnp.zeros((WIDE, LANES - WIDTH), BF)], 1
        )
    for copy in live_copies():
        copy.wait()
    total = jnp.zeros((blocks, LANES), F32)
    for g in range(4):
        pick = onehot(
            LANES,
            LANES,
            lambda a, b: (b % 4 == g) & (a == b - g + me),
        )
        total = total + dot(lived[g].astype(BF), pick, 1, 0)
    for i in range(chunks):
        dealt[i] = total[i * 4 : (i + 1) * 4]

    @pl.loop(0, chunks // 2)
    def _(i):
        qkv = project(wq[1], join(i, there, got, there_sems))
        part(i, answer, heard, answer_sems, attend(qkv, rows_of(dealt, i)))

    @pl.loop(0, chunks // 2)
    def _(i):
        state = states[i] + dot(wo[1], join(i, answer, heard, answer_sems), 1, 0)
        state = feed_forward(state, gains[:, 3:4], wi[1], back_ref[1])
        deal = cell_matrix()
        row = rows_of(lives, i)
        for b in range(8):
            fine = state[:, b * LANES : (b + 1) * LANES].astype(BF).astype(F32) * row[b]
            fine = jnp.concatenate([fine.astype(BF), jnp.zeros((LANES - WIDTH, LANES), BF)], 0)
            cell = dot(deal, fine, 1, 1).astype(BF)
            at = pl.ds(pl.multiple_of(i * (2 * CHUNK // PARENT) + b * 16, 16), 16)
            for c in range(PARENT):
                pooled[at, c * LANES : (c + 1) * LANES] = cell[c * 16 : (c + 1) * 16]

    fetch.wait()
    every = pooled[...]
    weight = wide[...]
    column_gain = gain[:, 0:1]
    pre = dot(weight, every, 1, 1)
    centered = pre - jnp.mean(pre, axis=0, keepdims=True)
    scale = lax.rsqrt(jnp.mean(centered * centered, axis=0, keepdims=True) + EPS)
    unit = centered * scale
    slope = cot[...].astype(F32) * column_gain
    slope = slope - jnp.mean(slope, axis=0, keepdims=True) - unit * jnp.mean(slope * unit, axis=0, keepdims=True)
    half = (slope * scale).astype(BF)
    order = [(1 - core) * 4, core * 4]
    for c in range(PARENT):
        term[c] = dot(half, every[:, c * LANES : (c + 1) * LANES], 1, 0).astype(BF)
    first = send(term.at[pl.ds(order[0], 4)], crossed, sems.at[0, 0], sems.at[1, 0], across)
    first.start()

    ours = pl.ds(pl.multiple_of(me * cells, LANES), cells)
    run_ref[:, ours] = (unit * column_gain).astype(BF)
    shares = []

    def share(pieces_now):
        for piece in pieces_now:
            lanes = pl.ds(pl.multiple_of(me * cells + piece // 2 * LANES, LANES), LANES)
            spot = run_ref.at[piece % 2 * WIDTH : piece % 2 * WIDTH + WIDTH, lanes]
            for d in (2, 1, 3):
                shares.append(
                    send(spot, spot, run_sems.at[0, piece, d - 1], run_sems.at[1, piece, d - 1], group[d - 1])
                )
                shares[-1].start()

    sent = [first]
    first.wait_recv()
    for i in range(4):
        summed[i] = (term[order[1] + i].astype(F32) + crossed[i].astype(F32)).astype(BF)
    moves = []
    for d in range(1, 4):
        moves.append(send(summed.at[(x + d) % 4], lines.at[d - 1], sems.at[0, d], sems.at[1, d], beside[d - 1]))
        moves[-1].start()
    share((0,))

    back = dot(half, weight, 0, 0).astype(BF)
    deal = cell_matrix()
    for b in range(blocks):
        cell = jnp.concatenate(
            [back[b * 16 : (b + 1) * 16, c * LANES : (c + 1) * LANES] for c in range(PARENT)], 0
        )
        fine = dot(cell, deal, 0, 0)[:WIDTH] * lives[b // 4, b % 4 : b % 4 + 1]
        fine_ref[:, b * LANES : (b + 1) * LANES] = fine.astype(BF)

    for move in moves:
        move.wait_recv()
    sent += moves
    total = summed[x].astype(F32)
    for d in range(3):
        total = total + lines[d].astype(F32)
    mine[:WIDE] = total.astype(BF)
    mine[WIDE:] = jnp.zeros((256 - WIDE, LANES), BF)
    moves = []
    for d in range(1, 8):
        to = pl.ds(pl.multiple_of((y + d) % 8 * 32, 32), 32)
        moves.append(send(mine.at[to], planes.at[d - 1], sems.at[0, 3 + d], sems.at[1, 3 + d], along[d - 1]))
        moves[-1].start()
    share((1, 2))
    for move in moves:
        move.wait_recv()
    sent += moves
    row = pl.ds(pl.multiple_of(y * 32, 32), 32)
    total = mine[row].astype(F32)
    for d in range(7):
        total = total + planes[d].astype(F32)
    pieces[z] = total.astype(BF)
    moves = []
    for d in range(1, 8):
        moves.append(send(pieces.at[z], pieces.at[z], sems.at[0, 10 + d], sems.at[1, 10 + d], above[d - 1]))
        moves[-1].start()
    share((3,))
    for move in moves:
        move.wait_recv()
    sent += moves
    total = pieces[0].astype(F32)
    for i in range(1, 8):
        total = total + pieces[i].astype(F32)
    column[row] = total.astype(BF)
    moves = []
    for d in range(1, 8):
        moves.append(send(column.at[row], column.at[row], sems.at[0, 17 + d], sems.at[1, 17 + d], along[d - 1]))
        moves[-1].start()
    share((4, 5))
    for move in moves:
        move.wait_recv()
    sent += moves
    spot = core * 4 + x
    whole[spot] = column[:WIDE]
    moves = []
    for d in range(1, 4):
        moves.append(send(whole.at[spot], whole.at[spot], sems.at[0, 24 + d], sems.at[1, 24 + d], beside[d - 1]))
        moves[-1].start()
    passed = [send(whole.at[spot], whole.at[spot], sems.at[0, 28], sems.at[1, 28], across)]
    passed[-1].start()

    for d in range(1, 4):
        moves[d - 1].wait_recv()
        here = core * 4 + (x - d + 4) % 4
        passed.append(send(whole.at[here], whole.at[here], sems.at[0, 28 + d], sems.at[1, 28 + d], across))
        passed[-1].start()
    for copy in passed:
        copy.wait_recv()
    sent += moves + passed
    for c in range(PARENT):
        grad_ref[:, c * WIDTH : (c + 1) * WIDTH] = whole[c][:, :WIDTH].astype(F32) * (
            1.0 / math.sqrt(lax.axis_size("slab") * run_ref.shape[1])
        )
    for copy in shares:
        copy.wait()
    for copy in sent:
        copy.wait_send()

    @pl.loop(0, chunks)
    def _(i):
        for copy in copies(i, there, got, there_sems) + copies(i, answer, heard, answer_sems):
            copy.wait_send()


def local(points, slot_mask, window_counts, block_gains, qkv_weight, out_weight, mlp_in, mlp_out, down_weight,
          coarse_gain, coarse_grad):
    rows = points.shape[2]
    blocks, cells, chunks = rows // LANES, rows // PARENT, rows // CHUNK
    vmem = pl.BlockSpec(memory_space=pltpu.VMEM)
    sems = pltpu.SemaphoreType.DMA
    run, fine, grad = pl.pallas_call(
        whole_kernel,
        in_specs=[vmem] * 8 + [pl.BlockSpec(memory_space=pl.ANY), vmem, pl.BlockSpec(memory_space=pl.ANY)],
        out_specs=[vmem] * 3,
        out_shape=[
            jax.ShapeDtypeStruct((WIDE, 4 * cells), BF),
            jax.ShapeDtypeStruct((WIDTH, rows), BF),
            jax.ShapeDtypeStruct((WIDE, PARENT * WIDTH), F32),
        ],
        scratch_shapes=[
            pltpu.VMEM((2, 3 * WIDTH, WIDTH), BF),
            pltpu.VMEM((2, WIDTH, WIDTH), BF),
            pltpu.VMEM((2, 4 * WIDTH, WIDTH), BF),
            pltpu.VMEM((WIDTH, 8), F32),
            pltpu.VMEM((WIDE, 8), F32),
            pltpu.VMEM((2, CHUNK, CHUNK), BF),
            pltpu.VMEM((WIDE, PARENT * LANES), BF),
            pltpu.VMEM((chunks // 2, WIDTH, 2 * CHUNK), F32),
            pltpu.VMEM((chunks, 4, LANES), F32),
            pltpu.VMEM((4, blocks, LANES), F32),
            pltpu.VMEM((chunks, 4, LANES), F32),
            pltpu.VMEM((chunks, 4, WIDTH, LANES), BF),
            pltpu.VMEM((chunks, 4, WIDTH, LANES), BF),
            pltpu.VMEM((chunks, 4, WIDTH, LANES), BF),
            pltpu.VMEM((chunks, 4, WIDTH, LANES), BF),
            pltpu.VMEM((cells, PARENT * LANES), BF),
            pltpu.VMEM((WIDE, cells), BF),
            pltpu.VMEM((WIDE, PARENT * WIDTH), BF),
            pltpu.VMEM((PARENT, WIDE, LANES), BF),
            pltpu.VMEM((4, WIDE, LANES), BF),
            pltpu.VMEM((4, WIDE, LANES), BF),
            pltpu.VMEM((3, WIDE, LANES), BF),
            pltpu.VMEM((256, LANES), BF),
            pltpu.VMEM((7, 32, LANES), BF),
            pltpu.VMEM((8, 32, LANES), BF),
            pltpu.VMEM((256, LANES), BF),
            pltpu.VMEM((8, WIDE, LANES), BF),
            sems,
            sems,
            sems((2, 3)),
            sems((2, chunks, 3)),
            sems((2, chunks, 3)),
            sems((2, 6, 3)),
            sems((2, 32)),
        ],
        compiler_params=pltpu.CompilerParams(
            collective_id=1, has_side_effects=True, vmem_limit_bytes=VMEM_LIMIT
        ),
    )(
        points.reshape(rows, WIDTH).T, slot_mask.reshape(blocks, LANES), window_counts, block_gains.reshape(4, WIDTH),
        qkv_weight, out_weight, mlp_in, jnp.swapaxes(mlp_out, 1, 2), down_weight.T, coarse_gain.reshape(1, WIDE),
        coarse_grad.reshape(4 * cells, WIDE).T,
    )
    return run.T.reshape(1, 4 * cells, WIDE), fine.T.reshape(1, 1, rows, WIDTH), grad.T


def solution(mesh):
    placed = (
        P("slab", "grp", None, None), P("slab", "grp", None), P("slab", "grp"), P(), P(), P(), P(), P(), P(), P(),
        P("slab", None, None),
    )
    return jax.shard_map(
        local,
        mesh=mesh,
        in_specs=placed,
        out_specs=(P("slab", None, None), P("slab", "grp", None, None), P()),
        check_vma=False,
    )
```

```python
import functools
import math

import jax
import jax.numpy as jnp
from jax import lax
from jax.experimental import pallas as pl
from jax.experimental.pallas import tpu as pltpu
from jax.sharding import PartitionSpec as P

MESH = pl.DeviceIdType.MESH
F32 = jnp.float32
BF = jnp.bfloat16
HEADS = 6
DEPTH = 16
WIDTH = 96
WINDOW = 32
LANES = 128
CHUNK = 512
PARENT = 8
WIDE = 192
EPS = 1e-05
NEG = -1e30
VMEM_LIMIT = 56 * 1024 * 1024


def dot(a, b, ca, cb):
    return lax.dot_general(a, b, (((ca,), (cb,)), ((), ())), preferred_element_type=F32)


def iota(shape, dim):
    return lax.broadcasted_iota(jnp.int32, shape, dim)


def onehot(rows, cols, match):
    return jnp.where(match(iota((rows, cols), 0), iota((rows, cols), 1)), 1.0, 0.0).astype(BF)


def cell_matrix():
    return onehot(LANES, LANES, lambda r, l: r % 16 * PARENT + r // 16 == l)


def norm_rows(value, gain):
    mean = jnp.mean(value, axis=0, keepdims=True)
    centered = value - mean
    spread = jnp.mean(centered * centered, axis=0, keepdims=True)
    return centered * lax.rsqrt(spread + EPS) * gain


def gelu(x):
    return 0.5 * x * (1.0 + lax.erf(x * (0.5**0.5)))


def lane_of(slot):
    return slot % 4 * LANES + slot // WINDOW * 8 + slot % WINDOW // 4


def key_mask(live_row):
    own = iota((WINDOW, LANES), 1) % WINDOW == iota((WINDOW, LANES), 0)
    spread = jnp.where(own, jnp.broadcast_to(live_row, (WINDOW, LANES)), 0.0).astype(BF)
    same = onehot(LANES, LANES, lambda a, b: a // WINDOW == b // WINDOW)
    return (dot(spread, same, 1, 0) > 0.5) | own


def attend(qkv_t, live):
    which = (iota((1, 2 * LANES), 1) % LANES) // WINDOW
    none = jnp.zeros((DEPTH, LANES), BF)
    zero = jnp.zeros((), BF)
    parts = [qkv_t[:, b * LANES : (b + 1) * LANES] for b in range(len(live))]
    keys = [jnp.transpose(p[WIDTH : 2 * WIDTH].astype(F32)).astype(BF) for p in parts]
    masks = [key_mask(row) for row in live]
    scores, spreads = {}, {}
    for b in range(len(live)):
        for pair in range(HEADS // 2):
            cols = []
            for h in (2 * pair, 2 * pair + 1):
                q = parts[b][h * DEPTH : (h + 1) * DEPTH]
                cols.append(jnp.concatenate([q if i == h else none for i in range(HEADS)], 0))
            scores[b, pair] = dot(keys[b], jnp.concatenate(cols, 1), 1, 0)
    for at, score in scores.items():
        s = score.reshape(4, WINDOW, 2 * LANES)
        folded = jnp.where(which == 0, s[0], jnp.where(which == 1, s[1], jnp.where(which == 2, s[2], s[3])))
        mask = masks[at[0]]
        folded = jnp.where(jnp.concatenate([mask, mask], 1), folded, NEG)
        expo = jnp.exp(folded - jnp.max(folded, axis=0, keepdims=True))
        scale = 1.0 / jnp.sum(expo, axis=0, keepdims=True)
        half = expo.astype(BF)
        spreads[at] = jnp.concatenate([jnp.where(which == w, half, zero) for w in range(4)], 0), scale
    outs = []
    for b in range(len(live)):
        rows = []
        for pair in range(HEADS // 2):
            spread, scale = spreads[b, pair]
            first = 2 * WIDTH + pair * 2 * DEPTH
            mixed = dot(parts[b][first : first + 2 * DEPTH], spread, 1, 0) * scale
            rows += [mixed[:DEPTH, :LANES], mixed[DEPTH:, LANES:]]
        outs.append(jnp.concatenate(rows, 0).astype(BF))
    return jnp.concatenate(outs, 1)


def project(w_t, normed):
    qkv = dot(w_t, normed, 1, 0)
    return jnp.concatenate([qkv[:WIDTH] * (DEPTH**-0.5), qkv[WIDTH:]], 0).astype(BF)


def feed_forward(state, gain, w_in_t, w_back_t):
    inner = norm_rows(state, gain).astype(BF)
    parts = [dot(w_in_t, inner[:, at : at + 256], 1, 0) for at in range(0, state.shape[1], 256)]
    backs = [dot(w_back_t, gelu(p).astype(BF), 1, 0) for p in parts]
    return state + jnp.concatenate(backs, 1)


def turn(w):
    return jnp.transpose(w.astype(F32)).astype(BF)


def axis_ids():
    slab, grp = lax.axis_index("slab"), lax.axis_index("grp")
    core, x, z_lo, y = slab % 2, (slab // 2) % 4, (slab // 8) % 2, slab // 16
    return core, x, y, grp * 2 + z_lo


def device_at(core, x, y, z):
    return {"slab": ((y * 2 + z % 2) * 4 + x) * 2 + core, "grp": z // 2}


def send(src, dst, send_sem, recv_sem, peer):
    return pltpu.make_async_remote_copy(
        src_ref=src, dst_ref=dst, send_sem=send_sem, recv_sem=recv_sem, device_id=peer, device_id_type=MESH
    )


def whole_kernel(
    points_ref, mask_ref, count_ref, gains_ref, qkv_ref, out_ref, in_ref, back_ref, weight_ref, gain_ref, cot_ref,
    run_ref, fine_ref, grad_ref,
    wq, wo, wi, gains, gain, swap, wide, states, lives, lived, dealt, there, got, answer, heard, pooled, cot, loaded, term,
    crossed, summed, lines, mine, planes, pieces, column, whole,
    cot_sem, load_sem, live_sems, there_sems, answer_sems, run_sems, sems,
):
    core, x, y, z = axis_ids()
    me = lax.axis_index("grp")
    slab = lax.axis_index("slab")
    chunks, cells = there.shape[0], pooled.shape[0]
    group = [{"slab": slab, "grp": (me + d) % 4} for d in (1, 2, 3)]
    across = device_at(1 - core, x, y, z)
    beside = [device_at(core, (x + d) % 4, y, z) for d in range(1, 4)]
    along = [device_at(core, x, (y + d) % 8, z) for d in range(1, 8)]
    above = [device_at(core, x, y, (z + d) % 8) for d in range(1, 8)]
    barrier = pltpu.get_barrier_semaphore()
    diagonal = [device_at(1 - core, (x + d) % 4, y, z) for d in range(1, 4)]
    peers = [across] + beside + diagonal + along + above
    for peer in peers:
        pl.semaphore_signal(barrier, inc=1, device_id=peer, device_id_type=MESH)

    fetch = pltpu.make_async_copy(cot_ref.at[:, pl.ds(pl.multiple_of(me * cells, LANES), cells)], cot, cot_sem)
    fetch.start()

    load = pltpu.make_async_copy(weight_ref, loaded, load_sem)
    load.start()

    wq[0] = turn(qkv_ref[0])
    wo[0] = turn(out_ref[0])
    wi[0] = turn(in_ref[0])
    gains[...] = jnp.transpose(jnp.concatenate([gains_ref[...], gains_ref[...]], 0))
    gain[...] = jnp.transpose(jnp.broadcast_to(gain_ref[...], (8, WIDE)))
    swap[0] = onehot(CHUNK, CHUNK, lambda a, b: lane_of(a) == b)
    swap[1] = onehot(CHUNK, CHUNK, lambda a, b: lane_of(b) == a)
    blocks = mask_ref.shape[0]
    window = iota((blocks, LANES), 0) * 4 + iota((blocks, LANES), 1) // WINDOW
    live = jnp.where(window < count_ref[...], mask_ref[...].astype(F32), 0.0)
    lived[me] = live
    for i in range(chunks):
        lives[i] = live[i * 4 : (i + 1) * 4]

    def live_copies():
        return [
            send(lived.at[me], lived.at[me], live_sems.at[0, d - 1], live_sems.at[1, d - 1], group[d - 1])
            for d in (2, 1, 3)
        ]

    def copies(i, src, dst, table):
        return [
            send(src.at[i, (me + d) % 4], dst.at[i, me], table.at[0, i, d - 1], table.at[1, i, d - 1], group[d - 1])
            for d in (2, 1, 3)
        ]

    def part(i, src, dst, table, rows):
        rows = dot(rows, swap[0], 1, 0).astype(BF)
        for r in range(4):
            src[i, r] = rows[:, r * LANES : (r + 1) * LANES]
        dst[i, me] = src[i, me]
        for copy in copies(i, src, dst, table):
            copy.start()

    def join(i, src, dst, table):
        for copy in copies(i, src, dst, table):
            copy.wait_recv()
        return dot(jnp.concatenate([dst[i, g] for g in range(4)], 1), swap[1], 1, 0).astype(BF)

    def rows_of(table, at):
        return [table[i][b : b + 1] for i in at for b in range(4)]

    @pl.loop(0, chunks // 2)
    def _(i):
        state = points_ref[:, pl.ds(pl.multiple_of(i * 2 * CHUNK, CHUNK), 2 * CHUNK)].astype(F32)
        qkv = project(wq[0], norm_rows(state, gains[:, 0:1]).astype(BF))
        state = state + dot(wo[0], attend(qkv, rows_of(lives, (2 * i, 2 * i + 1))), 1, 0)
        state = feed_forward(state, gains[:, 1:2], wi[0], back_ref[0])
        states[2 * i] = state[:, :CHUNK]
        states[2 * i + 1] = state[:, CHUNK:]
        normed = norm_rows(state, gains[:, 2:3]).astype(BF)

        @pl.when(i == 0)
        def _():
            pl.semaphore_wait(barrier, len(peers))
            for copy in live_copies():
                copy.start()

        part(2 * i, there, got, there_sems, normed[:, :CHUNK])
        part(2 * i + 1, there, got, there_sems, normed[:, CHUNK:])

    wq[1] = turn(qkv_ref[1])
    wo[1] = turn(out_ref[1])
    wi[1] = turn(in_ref[1])
    load.wait()
    for c in range(PARENT):
        wide[:, c * LANES : (c + 1) * LANES] = jnp.concatenate(
            [loaded[:, c * WIDTH : (c + 1) * WIDTH], jnp.zeros((WIDE, LANES - WIDTH), BF)], 1
        )
    for copy in live_copies():
        copy.wait()
    total = jnp.zeros((blocks, LANES), F32)
    for g in range(4):
        pick = onehot(
            LANES,
            LANES,
            lambda a, b: (b % 4 == g) & (a == b - g + me),
        )
        total = total + dot(lived[g].astype(BF), pick, 1, 0)
    for i in range(chunks):
        dealt[i] = total[i * 4 : (i + 1) * 4]

    @pl.loop(0, chunks)
    def _(i):
        qkv = project(wq[1], join(i, there, got, there_sems))
        part(i, answer, heard, answer_sems, attend(qkv, rows_of(dealt, (i,))))

    @pl.loop(0, chunks)
    def _(i):
        state = states[i] + dot(wo[1], join(i, answer, heard, answer_sems), 1, 0)
        state = feed_forward(state, gains[:, 3:4], wi[1], back_ref[1])
        deal = cell_matrix()
        row = rows_of(lives, (i,))
        for b in range(4):
            fine = state[:, b * LANES : (b + 1) * LANES].astype(BF).astype(F32) * row[b]
            fine = jnp.concatenate([fine.astype(BF), jnp.zeros((LANES - WIDTH, LANES), BF)], 0)
            cell = dot(deal, fine, 1, 1).astype(BF)
            at = pl.ds(pl.multiple_of(i * (CHUNK // PARENT) + b * 16, 16), 16)
            for c in range(PARENT):
                pooled[at, c * LANES : (c + 1) * LANES] = cell[c * 16 : (c + 1) * 16]

    fetch.wait()
    every = pooled[...]
    weight = wide[...]
    column_gain = gain[:, 0:1]
    pre = dot(weight, every, 1, 1)
    centered = pre - jnp.mean(pre, axis=0, keepdims=True)
    scale = lax.rsqrt(jnp.mean(centered * centered, axis=0, keepdims=True) + EPS)
    unit = centered * scale
    slope = cot[...].astype(F32) * column_gain
    slope = slope - jnp.mean(slope, axis=0, keepdims=True) - unit * jnp.mean(slope * unit, axis=0, keepdims=True)
    half = (slope * scale).astype(BF)
    order = [(1 - core) * 4, core * 4]
    for c in range(PARENT):
        term[c] = dot(half, every[:, c * LANES : (c + 1) * LANES], 1, 0).astype(BF)
    first = send(term.at[pl.ds(order[0], 4)], crossed, sems.at[0, 0], sems.at[1, 0], across)
    first.start()

    ours = pl.ds(pl.multiple_of(me * cells, LANES), cells)
    run_ref[:, ours] = (unit * column_gain).astype(BF)
    shares = []

    def share(pieces_now):
        for piece in pieces_now:
            lanes = pl.ds(pl.multiple_of(me * cells + piece // 2 * LANES, LANES), LANES)
            spot = run_ref.at[piece % 2 * WIDTH : piece % 2 * WIDTH + WIDTH, lanes]
            for d in (2, 1, 3):
                shares.append(
                    send(spot, spot, run_sems.at[0, piece, d - 1], run_sems.at[1, piece, d - 1], group[d - 1])
                )
                shares[-1].start()

    sent = [first]
    first.wait_recv()
    for i in range(4):
        summed[i] = (term[order[1] + i].astype(F32) + crossed[i].astype(F32)).astype(BF)
    moves = []
    for d in (2, 1, 3):
        moves.append(send(summed.at[(x + d) % 4], lines.at[d - 1], sems.at[0, d], sems.at[1, d], beside[d - 1]))
        moves[-1].start()
    share((0,))

    back = dot(half, weight, 0, 0).astype(BF)
    deal = cell_matrix()
    for b in range(blocks):
        cell = jnp.concatenate(
            [back[b * 16 : (b + 1) * 16, c * LANES : (c + 1) * LANES] for c in range(PARENT)], 0
        )
        fine = dot(cell, deal, 0, 0)[:WIDTH] * lives[b // 4, b % 4 : b % 4 + 1]
        fine_ref[:, b * LANES : (b + 1) * LANES] = fine.astype(BF)

    for move in moves:
        move.wait_recv()
    sent += moves
    total = summed[x].astype(F32)
    for d in range(3):
        total = total + lines[d].astype(F32)
    mine[:WIDE] = total.astype(BF)
    mine[WIDE:] = jnp.zeros((256 - WIDE, LANES), BF)
    moves = []
    for d in (4, 3, 5, 2, 6, 1, 7):
        to = pl.ds(pl.multiple_of((y + d) % 8 * 32, 32), 32)
        moves.append(send(mine.at[to], planes.at[d - 1], sems.at[0, 3 + d], sems.at[1, 3 + d], along[d - 1]))
        moves[-1].start()
    share((1, 2))
    for move in moves:
        move.wait_recv()
    sent += moves
    row = pl.ds(pl.multiple_of(y * 32, 32), 32)
    total = mine[row].astype(F32)
    for d in range(7):
        total = total + planes[d].astype(F32)
    pieces[z] = total.astype(BF)
    moves = []
    for d in (4, 3, 5, 2, 6, 1, 7):
        moves.append(send(pieces.at[z], pieces.at[z], sems.at[0, 10 + d], sems.at[1, 10 + d], above[d - 1]))
        moves[-1].start()
    share((3,))
    for move in moves:
        move.wait_recv()
    sent += moves
    total = pieces[0].astype(F32)
    for i in range(1, 8):
        total = total + pieces[i].astype(F32)
    column[row] = total.astype(BF)
    moves = []
    for d in (4, 3, 5, 2, 6, 1, 7):
        moves.append(send(column.at[row], column.at[row], sems.at[0, 17 + d], sems.at[1, 17 + d], along[d - 1]))
        moves[-1].start()
    share((4, 5))
    for move in moves:
        move.wait_recv()
    sent += moves
    spot = core * 4 + x
    whole[spot] = column[:WIDE]
    moves = []
    for d in (2, 1, 3):
        for other in range(2):
            at = 24 + d * 2 + other
            peer = device_at((core + other) % 2, (x + d) % 4, y, z)
            moves.append(send(whole.at[spot], whole.at[spot], sems.at[0, at], sems.at[1, at], peer))
            moves[-1].start()
    moves.append(send(whole.at[spot], whole.at[spot], sems.at[0, 25], sems.at[1, 25], across))
    moves[-1].start()
    for move in moves:
        move.wait_recv()
    sent += moves
    for c in range(PARENT):
        grad_ref[:, c * WIDTH : (c + 1) * WIDTH] = whole[c][:, :WIDTH].astype(F32) * (
            1.0 / math.sqrt(lax.axis_size("slab") * run_ref.shape[1])
        )
    for copy in shares:
        copy.wait()
    for copy in sent:
        copy.wait_send()

    @pl.loop(0, chunks)
    def _(i):
        for copy in copies(i, there, got, there_sems) + copies(i, answer, heard, answer_sems):
            copy.wait_send()


def leave_kernel(run_ref, fine_ref, grad_ref, run_out, fine_out, grad_out, sems):
    pairs = ((run_ref, run_out), (fine_ref, fine_out), (grad_ref, grad_out))
    moves = [pltpu.make_async_copy(a, b, sems.at[i]) for i, (a, b) in enumerate(pairs)]
    for move in moves:
        move.start()
    for move in moves:
        move.wait()


def local(points, slot_mask, window_counts, block_gains, qkv_weight, out_weight, mlp_in, mlp_out, down_weight,
          coarse_gain, coarse_grad):
    rows = points.shape[2]
    blocks, cells, chunks = rows // LANES, rows // PARENT, rows // CHUNK
    vmem = pl.BlockSpec(memory_space=pltpu.VMEM)
    sems = pltpu.SemaphoreType.DMA
    run, fine, grad = pl.pallas_call(
        whole_kernel,
        in_specs=[vmem] * 8 + [pl.BlockSpec(memory_space=pl.ANY), vmem, pl.BlockSpec(memory_space=pl.ANY)],
        out_specs=[vmem] * 3,
        out_shape=[
            pltpu.VMEM((WIDE, 4 * cells), BF),
            pltpu.VMEM((WIDTH, rows), BF),
            pltpu.VMEM((WIDE, PARENT * WIDTH), F32),
        ],
        scratch_shapes=[
            pltpu.VMEM((2, 3 * WIDTH, WIDTH), BF),
            pltpu.VMEM((2, WIDTH, WIDTH), BF),
            pltpu.VMEM((2, 4 * WIDTH, WIDTH), BF),
            pltpu.VMEM((WIDTH, 8), F32),
            pltpu.VMEM((WIDE, 8), F32),
            pltpu.VMEM((2, CHUNK, CHUNK), BF),
            pltpu.VMEM((WIDE, PARENT * LANES), BF),
            pltpu.VMEM((chunks, WIDTH, CHUNK), F32),
            pltpu.VMEM((chunks, 4, LANES), F32),
            pltpu.VMEM((4, blocks, LANES), F32),
            pltpu.VMEM((chunks, 4, LANES), F32),
            pltpu.VMEM((chunks, 4, WIDTH, LANES), BF),
            pltpu.VMEM((chunks, 4, WIDTH, LANES), BF),
            pltpu.VMEM((chunks, 4, WIDTH, LANES), BF),
            pltpu.VMEM((chunks, 4, WIDTH, LANES), BF),
            pltpu.VMEM((cells, PARENT * LANES), BF),
            pltpu.VMEM((WIDE, cells), BF),
            pltpu.VMEM((WIDE, PARENT * WIDTH), BF),
            pltpu.VMEM((PARENT, WIDE, LANES), BF),
            pltpu.VMEM((4, WIDE, LANES), BF),
            pltpu.VMEM((4, WIDE, LANES), BF),
            pltpu.VMEM((3, WIDE, LANES), BF),
            pltpu.VMEM((256, LANES), BF),
            pltpu.VMEM((7, 32, LANES), BF),
            pltpu.VMEM((8, 32, LANES), BF),
            pltpu.VMEM((256, LANES), BF),
            pltpu.VMEM((8, WIDE, LANES), BF),
            sems,
            sems,
            sems((2, 3)),
            sems((2, chunks, 3)),
            sems((2, chunks, 3)),
            sems((2, 6, 3)),
            sems((2, 32)),
        ],
        compiler_params=pltpu.CompilerParams(
            collective_id=1, has_side_effects=True, vmem_limit_bytes=VMEM_LIMIT
        ),
    )(
        points.reshape(rows, WIDTH).T, slot_mask.reshape(blocks, LANES), window_counts, block_gains.reshape(4, WIDTH),
        qkv_weight, out_weight, mlp_in, jnp.swapaxes(mlp_out, 1, 2), down_weight.T, coarse_gain.reshape(1, WIDE),
        coarse_grad.reshape(4 * cells, WIDE).T,
    )
    run, fine, grad = pl.pallas_call(
        leave_kernel,
        in_specs=[vmem] * 3,
        out_specs=[pl.BlockSpec(memory_space=pl.ANY)] * 3,
        out_shape=[jax.ShapeDtypeStruct(v.shape, v.dtype) for v in (run, fine, grad)],
        scratch_shapes=[sems((3,))],
        compiler_params=pltpu.CompilerParams(vmem_limit_bytes=VMEM_LIMIT),
    )(*[pltpu.with_memory_space_constraint(v, pltpu.VMEM) for v in (run, fine, grad)])
    return run.T.reshape(1, 4 * cells, WIDE), fine.T.reshape(1, 1, rows, WIDTH), grad.T


def solution(mesh):
    placed = (
        P("slab", "grp", None, None), P("slab", "grp", None), P("slab", "grp"), P(), P(), P(), P(), P(), P(), P(),
        P("slab", None, None),
    )
    return jax.shard_map(
        local,
        mesh=mesh,
        in_specs=placed,
        out_specs=(P("slab", None, None), P("slab", "grp", None, None), P()),
        check_vma=False,
    )
```

```python
import functools
import math

import jax
import jax.numpy as jnp
from jax import lax
from jax.experimental import pallas as pl
from jax.experimental.pallas import tpu as pltpu
from jax.sharding import PartitionSpec as P

MESH = pl.DeviceIdType.MESH
F32 = jnp.float32
BF = jnp.bfloat16
HEADS = 6
DEPTH = 16
WIDTH = 96
WINDOW = 32
LANES = 128
CHUNK = 512
PARENT = 8
WIDE = 192
EPS = 1e-05
NEG = -1e30
VMEM_LIMIT = 56 * 1024 * 1024


def dot(a, b, ca, cb):
    return lax.dot_general(a, b, (((ca,), (cb,)), ((), ())), preferred_element_type=F32)


def iota(shape, dim):
    return lax.broadcasted_iota(jnp.int32, shape, dim)


def onehot(rows, cols, match):
    return jnp.where(match(iota((rows, cols), 0), iota((rows, cols), 1)), 1.0, 0.0).astype(BF)


def cell_matrix():
    return onehot(LANES, LANES, lambda r, l: r % 16 * PARENT + r // 16 == l)


def norm_rows(value, gain):
    mean = jnp.mean(value, axis=0, keepdims=True)
    centered = value - mean
    spread = jnp.mean(centered * centered, axis=0, keepdims=True)
    return centered * lax.rsqrt(spread + EPS) * gain


def gelu(x):
    return 0.5 * x * (1.0 + lax.erf(x * (0.5**0.5)))


def lane_of(slot):
    return slot % 4 * LANES + slot // WINDOW * 8 + slot % WINDOW // 4


def key_mask(live_row):
    own = iota((WINDOW, LANES), 1) % WINDOW == iota((WINDOW, LANES), 0)
    spread = jnp.where(own, jnp.broadcast_to(live_row, (WINDOW, LANES)), 0.0).astype(BF)
    same = onehot(LANES, LANES, lambda a, b: a // WINDOW == b // WINDOW)
    return (dot(spread, same, 1, 0) > 0.5) | own


def attend(qkv_t, live):
    which = (iota((1, 2 * LANES), 1) % LANES) // WINDOW
    none = jnp.zeros((DEPTH, LANES), BF)
    zero = jnp.zeros((), BF)
    parts = [qkv_t[:, b * LANES : (b + 1) * LANES] for b in range(len(live))]
    keys = [jnp.transpose(p[WIDTH : 2 * WIDTH].astype(F32)).astype(BF) for p in parts]
    masks = [key_mask(row) for row in live]
    scores, spreads = {}, {}
    for b in range(len(live)):
        for pair in range(HEADS // 2):
            cols = []
            for h in (2 * pair, 2 * pair + 1):
                q = parts[b][h * DEPTH : (h + 1) * DEPTH]
                cols.append(jnp.concatenate([q if i == h else none for i in range(HEADS)], 0))
            scores[b, pair] = dot(keys[b], jnp.concatenate(cols, 1), 1, 0)
    for at, score in scores.items():
        s = score.reshape(4, WINDOW, 2 * LANES)
        folded = jnp.where(which == 0, s[0], jnp.where(which == 1, s[1], jnp.where(which == 2, s[2], s[3])))
        mask = masks[at[0]]
        folded = jnp.where(jnp.concatenate([mask, mask], 1), folded, NEG)
        expo = jnp.exp(folded - jnp.max(folded, axis=0, keepdims=True))
        scale = 1.0 / jnp.sum(expo, axis=0, keepdims=True)
        half = expo.astype(BF)
        spreads[at] = jnp.concatenate([jnp.where(which == w, half, zero) for w in range(4)], 0), scale
    outs = []
    for b in range(len(live)):
        rows = []
        for pair in range(HEADS // 2):
            spread, scale = spreads[b, pair]
            first = 2 * WIDTH + pair * 2 * DEPTH
            mixed = dot(parts[b][first : first + 2 * DEPTH], spread, 1, 0) * scale
            rows += [mixed[:DEPTH, :LANES], mixed[DEPTH:, LANES:]]
        outs.append(jnp.concatenate(rows, 0).astype(BF))
    return jnp.concatenate(outs, 1)


def project(w_t, normed):
    qkv = dot(w_t, normed, 1, 0)
    return jnp.concatenate([qkv[:WIDTH] * (DEPTH**-0.5), qkv[WIDTH:]], 0).astype(BF)


def feed_forward(state, gain, w_in_t, w_back_t):
    inner = norm_rows(state, gain).astype(BF)
    parts = [dot(w_in_t, inner[:, at : at + 256], 1, 0) for at in range(0, state.shape[1], 256)]
    backs = [dot(w_back_t, gelu(p).astype(BF), 1, 0) for p in parts]
    return state + jnp.concatenate(backs, 1)


def turn(w):
    return jnp.transpose(w.astype(F32)).astype(BF)


def axis_ids():
    slab, grp = lax.axis_index("slab"), lax.axis_index("grp")
    core, x, z_lo, y = slab % 2, (slab // 2) % 4, (slab // 8) % 2, slab // 16
    return core, x, y, grp * 2 + z_lo


def device_at(core, x, y, z):
    return {"slab": ((y * 2 + z % 2) * 4 + x) * 2 + core, "grp": z // 2}


def send(src, dst, send_sem, recv_sem, peer):
    return pltpu.make_async_remote_copy(
        src_ref=src, dst_ref=dst, send_sem=send_sem, recv_sem=recv_sem, device_id=peer, device_id_type=MESH
    )


def whole_kernel(
    points_ref, mask_ref, count_ref, gains_ref, qkv_ref, out_ref, in_ref, back_ref, weight_ref, gain_ref, cot_ref,
    run_ref, fine_ref, grad_ref,
    wq, wo, wi, gains, gain, swap, wide, states, lives, lived, dealt, there, got, answer, heard, pooled, cot, loaded, term,
    crossed, summed, lines, mine, planes, pieces, column, whole,
    cot_sem, load_sem, live_sems, there_sems, answer_sems, run_sems, sems,
):
    core, x, y, z = axis_ids()
    me = lax.axis_index("grp")
    slab = lax.axis_index("slab")
    chunks, cells = there.shape[0], pooled.shape[0]
    group = [{"slab": slab, "grp": (me + d) % 4} for d in (1, 2, 3)]
    across = device_at(1 - core, x, y, z)
    beside = [device_at(core, (x + d) % 4, y, z) for d in range(1, 4)]
    along = [device_at(core, x, (y + d) % 8, z) for d in range(1, 8)]
    above = [device_at(core, x, y, (z + d) % 8) for d in range(1, 8)]
    barrier = pltpu.get_barrier_semaphore()
    diagonal = [device_at(1 - core, (x + d) % 4, y, z) for d in range(1, 4)]
    peers = [across] + beside + diagonal + along + above
    for peer in peers:
        pl.semaphore_signal(barrier, inc=1, device_id=peer, device_id_type=MESH)

    fetch = pltpu.make_async_copy(cot_ref.at[:, pl.ds(pl.multiple_of(me * cells, LANES), cells)], cot, cot_sem)
    fetch.start()

    load = pltpu.make_async_copy(weight_ref, loaded, load_sem)
    load.start()

    wq[0] = turn(qkv_ref[0])
    wo[0] = turn(out_ref[0])
    wi[0] = turn(in_ref[0])
    gains[...] = jnp.transpose(jnp.concatenate([gains_ref[...], gains_ref[...]], 0))
    gain[...] = jnp.transpose(jnp.broadcast_to(gain_ref[...], (8, WIDE)))
    swap[0] = onehot(CHUNK, CHUNK, lambda a, b: lane_of(a) == b)
    swap[1] = onehot(CHUNK, CHUNK, lambda a, b: lane_of(b) == a)
    blocks = mask_ref.shape[0]
    window = iota((blocks, LANES), 0) * 4 + iota((blocks, LANES), 1) // WINDOW
    live = jnp.where(window < count_ref[...], mask_ref[...].astype(F32), 0.0)
    lived[me] = live
    for i in range(chunks):
        lives[i] = live[i * 4 : (i + 1) * 4]

    def live_copies():
        return [
            send(lived.at[me], lived.at[me], live_sems.at[0, d - 1], live_sems.at[1, d - 1], group[d - 1])
            for d in (2, 1, 3)
        ]

    def copies(i, src, dst, table):
        return [
            send(src.at[i, (me + d) % 4], dst.at[i, me], table.at[0, i, d - 1], table.at[1, i, d - 1], group[d - 1])
            for d in (2, 1, 3)
        ]

    def part(i, src, dst, table, rows):
        rows = dot(rows, swap[0], 1, 0).astype(BF)
        for r in range(4):
            src[i, r] = rows[:, r * LANES : (r + 1) * LANES]
        dst[i, me] = src[i, me]
        for copy in copies(i, src, dst, table):
            copy.start()

    def join(i, src, dst, table):
        for copy in copies(i, src, dst, table):
            copy.wait_recv()
        return dot(jnp.concatenate([dst[i, g] for g in range(4)], 1), swap[1], 1, 0).astype(BF)

    def rows_of(table, at):
        return [table[i][b : b + 1] for i in at for b in range(4)]

    @pl.loop(0, chunks)
    def _(i):
        state = points_ref[:, pl.ds(pl.multiple_of(i * CHUNK, CHUNK), CHUNK)].astype(F32)
        qkv = project(wq[0], norm_rows(state, gains[:, 0:1]).astype(BF))
        state = state + dot(wo[0], attend(qkv, rows_of(lives, (i,))), 1, 0)
        state = feed_forward(state, gains[:, 1:2], wi[0], back_ref[0])
        states[i] = state
        normed = norm_rows(state, gains[:, 2:3]).astype(BF)

        @pl.when(i == 0)
        def _():
            pl.semaphore_wait(barrier, len(peers))
            for copy in live_copies():
                copy.start()

        part(i, there, got, there_sems, normed)

    wq[1] = turn(qkv_ref[1])
    wo[1] = turn(out_ref[1])
    wi[1] = turn(in_ref[1])
    load.wait()
    for c in range(PARENT):
        wide[:, c * LANES : (c + 1) * LANES] = jnp.concatenate(
            [loaded[:, c * WIDTH : (c + 1) * WIDTH], jnp.zeros((WIDE, LANES - WIDTH), BF)], 1
        )
    for copy in live_copies():
        copy.wait()
    total = jnp.zeros((blocks, LANES), F32)
    for g in range(4):
        pick = onehot(
            LANES,
            LANES,
            lambda a, b: (b % 4 == g) & (a == b - g + me),
        )
        total = total + dot(lived[g].astype(BF), pick, 1, 0)
    for i in range(chunks):
        dealt[i] = total[i * 4 : (i + 1) * 4]

    @pl.loop(0, chunks)
    def _(i):
        qkv = project(wq[1], join(i, there, got, there_sems))
        part(i, answer, heard, answer_sems, attend(qkv, rows_of(dealt, (i,))))

    @pl.loop(0, chunks)
    def _(i):
        state = states[i] + dot(wo[1], join(i, answer, heard, answer_sems), 1, 0)
        state = feed_forward(state, gains[:, 3:4], wi[1], back_ref[1])
        deal = cell_matrix()
        row = rows_of(lives, (i,))
        for b in range(4):
            fine = state[:, b * LANES : (b + 1) * LANES].astype(BF).astype(F32) * row[b]
            fine = jnp.concatenate([fine.astype(BF), jnp.zeros((LANES - WIDTH, LANES), BF)], 0)
            cell = dot(deal, fine, 1, 1).astype(BF)
            at = pl.ds(pl.multiple_of(i * (CHUNK // PARENT) + b * 16, 16), 16)
            for c in range(PARENT):
                pooled[at, c * LANES : (c + 1) * LANES] = cell[c * 16 : (c + 1) * 16]

    fetch.wait()
    every = pooled[...]
    weight = wide[...]
    column_gain = gain[:, 0:1]
    pre = dot(weight, every, 1, 1)
    centered = pre - jnp.mean(pre, axis=0, keepdims=True)
    scale = lax.rsqrt(jnp.mean(centered * centered, axis=0, keepdims=True) + EPS)
    unit = centered * scale
    slope = cot[...].astype(F32) * column_gain
    slope = slope - jnp.mean(slope, axis=0, keepdims=True) - unit * jnp.mean(slope * unit, axis=0, keepdims=True)
    half = (slope * scale).astype(BF)
    order = [(1 - core) * 4, core * 4]
    for c in range(PARENT):
        term[c] = dot(half, every[:, c * LANES : (c + 1) * LANES], 1, 0).astype(BF)
    first = send(term.at[pl.ds(order[0], 4)], crossed, sems.at[0, 0], sems.at[1, 0], across)
    first.start()

    ours = pl.ds(pl.multiple_of(me * cells, LANES), cells)
    run_ref[:, ours] = (unit * column_gain).astype(BF)
    shares = []

    def share(pieces_now):
        for piece in pieces_now:
            lanes = pl.ds(pl.multiple_of(me * cells + piece // 2 * LANES, LANES), LANES)
            spot = run_ref.at[piece % 2 * WIDTH : piece % 2 * WIDTH + WIDTH, lanes]
            for d in (2, 1, 3):
                shares.append(
                    send(spot, spot, run_sems.at[0, piece, d - 1], run_sems.at[1, piece, d - 1], group[d - 1])
                )
                shares[-1].start()

    sent = [first]
    first.wait_recv()
    for i in range(4):
        summed[i] = (term[order[1] + i].astype(F32) + crossed[i].astype(F32)).astype(BF)
    moves = []
    for d in (2, 1, 3):
        moves.append(send(summed.at[(x + d) % 4], lines.at[d - 1], sems.at[0, d], sems.at[1, d], beside[d - 1]))
        moves[-1].start()
    share((0,))

    back = dot(half, weight, 0, 0).astype(BF)
    deal = cell_matrix()
    for b in range(blocks):
        cell = jnp.concatenate(
            [back[b * 16 : (b + 1) * 16, c * LANES : (c + 1) * LANES] for c in range(PARENT)], 0
        )
        fine = dot(cell, deal, 0, 0)[:WIDTH] * lives[b // 4, b % 4 : b % 4 + 1]
        fine_ref[:, b * LANES : (b + 1) * LANES] = fine.astype(BF)

    for move in moves:
        move.wait()
    total = summed[x].astype(F32)
    for d in range(3):
        total = total + lines[d].astype(F32)
    mine[:WIDE] = total.astype(BF)
    mine[WIDE:] = jnp.zeros((256 - WIDE, LANES), BF)
    moves = []
    for d in (4, 3, 5, 2, 6, 1, 7):
        to = pl.ds(pl.multiple_of((y + d) % 8 * 32, 32), 32)
        moves.append(send(mine.at[to], planes.at[d - 1], sems.at[0, 3 + d], sems.at[1, 3 + d], along[d - 1]))
        moves[-1].start()
    share((1, 2))
    for move in moves:
        move.wait()
    row = pl.ds(pl.multiple_of(y * 32, 32), 32)
    total = mine[row].astype(F32)
    for d in range(7):
        total = total + planes[d].astype(F32)
    pieces[z] = total.astype(BF)
    moves = []
    for d in (4, 3, 5, 2, 6, 1, 7):
        moves.append(send(pieces.at[z], pieces.at[z], sems.at[0, 10 + d], sems.at[1, 10 + d], above[d - 1]))
        moves[-1].start()
    share((3,))
    for move in moves:
        move.wait()
    total = pieces[0].astype(F32)
    for i in range(1, 8):
        total = total + pieces[i].astype(F32)
    column[row] = total.astype(BF)
    moves = []
    for d in (4, 3, 5, 2, 6, 1, 7):
        moves.append(send(column.at[row], column.at[row], sems.at[0, 17 + d], sems.at[1, 17 + d], along[d - 1]))
        moves[-1].start()
    share((4, 5))
    for move in moves:
        move.wait()
    spot = core * 4 + x
    whole[spot] = column[:WIDE]
    moves = []
    for d in (2, 1, 3):
        for other in range(2):
            at = 24 + d * 2 + other
            peer = device_at((core + other) % 2, (x + d) % 4, y, z)
            moves.append(send(whole.at[spot], whole.at[spot], sems.at[0, at], sems.at[1, at], peer))
            moves[-1].start()
    moves.append(send(whole.at[spot], whole.at[spot], sems.at[0, 25], sems.at[1, 25], across))
    moves[-1].start()
    for move in moves:
        move.wait()
    for c in range(PARENT):
        grad_ref[:, c * WIDTH : (c + 1) * WIDTH] = whole[c][:, :WIDTH].astype(F32) * (
            1.0 / math.sqrt(lax.axis_size("slab") * run_ref.shape[1])
        )
    for copy in shares:
        copy.wait()
    for copy in sent:
        copy.wait_send()

    @pl.loop(0, chunks)
    def _(i):
        for copy in copies(i, there, got, there_sems) + copies(i, answer, heard, answer_sems):
            copy.wait_send()


def leave_kernel(run_ref, fine_ref, grad_ref, run_out, fine_out, grad_out, sems):
    pairs = ((run_ref, run_out), (fine_ref, fine_out), (grad_ref, grad_out))
    moves = [pltpu.make_async_copy(a, b, sems.at[i]) for i, (a, b) in enumerate(pairs)]
    for move in moves:
        move.start()
    for move in moves:
        move.wait()


def local(points, slot_mask, window_counts, block_gains, qkv_weight, out_weight, mlp_in, mlp_out, down_weight,
          coarse_gain, coarse_grad):
    rows = points.shape[2]
    blocks, cells, chunks = rows // LANES, rows // PARENT, rows // CHUNK
    vmem = pl.BlockSpec(memory_space=pltpu.VMEM)
    sems = pltpu.SemaphoreType.DMA
    run, fine, grad = pl.pallas_call(
        whole_kernel,
        in_specs=[vmem] * 8 + [pl.BlockSpec(memory_space=pl.ANY), vmem, pl.BlockSpec(memory_space=pl.ANY)],
        out_specs=[vmem] * 3,
        out_shape=[
            pltpu.VMEM((WIDE, 4 * cells), BF),
            pltpu.VMEM((WIDTH, rows), BF),
            pltpu.VMEM((WIDE, PARENT * WIDTH), F32),
        ],
        scratch_shapes=[
            pltpu.VMEM((2, 3 * WIDTH, WIDTH), BF),
            pltpu.VMEM((2, WIDTH, WIDTH), BF),
            pltpu.VMEM((2, 4 * WIDTH, WIDTH), BF),
            pltpu.VMEM((WIDTH, 8), F32),
            pltpu.VMEM((WIDE, 8), F32),
            pltpu.VMEM((2, CHUNK, CHUNK), BF),
            pltpu.VMEM((WIDE, PARENT * LANES), BF),
            pltpu.VMEM((chunks, WIDTH, CHUNK), F32),
            pltpu.VMEM((chunks, 4, LANES), F32),
            pltpu.VMEM((4, blocks, LANES), F32),
            pltpu.VMEM((chunks, 4, LANES), F32),
            pltpu.VMEM((chunks, 4, WIDTH, LANES), BF),
            pltpu.VMEM((chunks, 4, WIDTH, LANES), BF),
            pltpu.VMEM((chunks, 4, WIDTH, LANES), BF),
            pltpu.VMEM((chunks, 4, WIDTH, LANES), BF),
            pltpu.VMEM((cells, PARENT * LANES), BF),
            pltpu.VMEM((WIDE, cells), BF),
            pltpu.VMEM((WIDE, PARENT * WIDTH), BF),
            pltpu.VMEM((PARENT, WIDE, LANES), BF),
            pltpu.VMEM((4, WIDE, LANES), BF),
            pltpu.VMEM((4, WIDE, LANES), BF),
            pltpu.VMEM((3, WIDE, LANES), BF),
            pltpu.VMEM((256, LANES), BF),
            pltpu.VMEM((7, 32, LANES), BF),
            pltpu.VMEM((8, 32, LANES), BF),
            pltpu.VMEM((256, LANES), BF),
            pltpu.VMEM((8, WIDE, LANES), BF),
            sems,
            sems,
            sems((2, 3)),
            sems((2, chunks, 3)),
            sems((2, chunks, 3)),
            sems((2, 6, 3)),
            sems((2, 32)),
        ],
        compiler_params=pltpu.CompilerParams(
            collective_id=1, has_side_effects=True, vmem_limit_bytes=VMEM_LIMIT
        ),
    )(
        points.reshape(rows, WIDTH).T, slot_mask.reshape(blocks, LANES), window_counts, block_gains.reshape(4, WIDTH),
        qkv_weight, out_weight, mlp_in, jnp.swapaxes(mlp_out, 1, 2), down_weight.T, coarse_gain.reshape(1, WIDE),
        coarse_grad.reshape(4 * cells, WIDE).T,
    )
    run, fine, grad = pl.pallas_call(
        leave_kernel,
        in_specs=[vmem] * 3,
        out_specs=[pl.BlockSpec(memory_space=pl.ANY)] * 3,
        out_shape=[jax.ShapeDtypeStruct(v.shape, v.dtype) for v in (run, fine, grad)],
        scratch_shapes=[sems((3,))],
        compiler_params=pltpu.CompilerParams(vmem_limit_bytes=VMEM_LIMIT),
    )(*[pltpu.with_memory_space_constraint(v, pltpu.VMEM) for v in (run, fine, grad)])
    return run.T.reshape(1, 4 * cells, WIDE), fine.T.reshape(1, 1, rows, WIDTH), grad.T


def solution(mesh):
    placed = (
        P("slab", "grp", None, None), P("slab", "grp", None), P("slab", "grp"), P(), P(), P(), P(), P(), P(), P(),
        P("slab", None, None),
    )
    return jax.shard_map(
        local,
        mesh=mesh,
        in_specs=placed,
        out_specs=(P("slab", None, None), P("slab", "grp", None, None), P()),
        check_vma=False,
    )
```
